32 devices in a mesh: zt: 16 (over z, x, core), xy: 2 (over y).
Axes of the slice: x: 2, y: 2, z: 4, core: 2. Of those that a mesh axis runs over, the one named last changes fastest.
Arguments:
- fine_vectors: bfloat16 [64, 2, 12, 16, 512], P('zt', None, None, None, 'xy'), may hold values from -6 to 6
- null_vectors: bfloat16 [64, 2, 12, 32, 512], P('zt', None, None, None, 'xy'), may hold values from -0.75 to 0.75
- coarse_operator: bfloat16 [16, 9, 2, 2, 2, 128, 128], P('zt'), may hold values from -0.3125 to 0.3125
Outputs:
- fine_correction: bfloat16 [64, 2, 12, 16, 512], P('zt', None, None, None, 'xy')
- coarse_iterate: bfloat16 [16, 2, 2, 2, 16, 128], P('zt')
The draws below stay inside these ranges and needn't reach their ends.
All inputs are finite; a program needn't handle non-finite values.
Results may differ from the reference program's by a relative error of at most 0.018.
Values may be sent and summed in bfloat16 or wider, within the bound.
No kernel may reach another device: no remote copies, remote signals or barrier semaphores. Data moves between devices by JAX's collectives and lax.ppermute only.
A program may use at most 128 MiB of HBM per device.

```python
import jax
import jax.numpy as jnp
from jax import lax

NV = 32
DOF = 128
RHS = 16
CZ = 2
CY = 2
APPLIES = 4
CT = 16
CX = 2
FT = 64
FX = 8
FZY = 64


def level_of(key, extent, cuts, smallest, high):
    level = 1.0
    for position, shards_of in cuts:
        steps = jax.random.uniform(jax.random.fold_in(jax.random.fold_in(key, 6), position), (shards_of,), jnp.float32, smallest / len(cuts), high / len(cuts))
        level = level * jnp.repeat(jnp.exp(steps), extent[position] // shards_of).reshape((-1,) + (1,) * (len(extent) - 1 - position))
    return level


def normal_values(rng, dims, width, limit, cuts=(), held_as=jnp.bfloat16):
    gain = level_of(rng, dims, cuts, -0.22, 0.18) if cuts else 1.0
    entries = jax.random.normal(rng, dims, jnp.float32) * width * gain
    return jnp.minimum(jnp.maximum(entries, -limit), limit).astype(held_as)


def setup_inputs(seed: int = 0) -> dict:
    keys = jax.random.split(jax.random.key(seed), 4)
    return {
        "fine_vectors": normal_values(keys[0], (FT, 2, 12, RHS, FX * FZY), 1.0, 6.0, ((0, 16), (4, 2))),
        "null_vectors": normal_values(keys[1], (FT, 2, 12, NV, FX * FZY), (2 * NV) ** -0.5, 0.75, ((0, 16), (4, 2))),
        "coarse_operator": normal_values(keys[2], (CT, 9, CY, CZ, CX, DOF, DOF), (3 * DOF) ** -0.5, 0.3125, ((0, 16),)),
    }


RELAX_WEIGHT = 0.3
DIAGONAL_SHIFT = 3.0


def restrict_slice(fine_slice, null_slice):
    rhs_count = fine_slice.shape[3]
    vectors = null_slice.shape[3]
    fine_view = fine_slice.astype(jnp.float32).reshape(4, 2, 2, 6, rhs_count, CX, 4, CZ, 4, CY, 4)
    null_view = null_slice.astype(jnp.float32).reshape(4, 2, 2, 6, vectors, CX, 4, CZ, 4, CY, 4)
    turned = jnp.stack([fine_view[:, 1], -fine_view[:, 0]], axis=1)
    real_sum = jnp.einsum("tqhgkcxzayb,tqhgrcxzayb->yzcrhk", null_view, fine_view)
    imag_sum = jnp.einsum("tqhgkcxzayb,tqhgrcxzayb->yzcrhk", null_view, turned)
    stacked = jnp.stack([real_sum, imag_sum], axis=4)
    return stacked.reshape(CY, CZ, CX, rhs_count, 4 * vectors)


def prolong_slice(coarse_slice, null_slice):
    rhs_count = coarse_slice.shape[3]
    vectors = coarse_slice.shape[4] // 4
    weights = coarse_slice.astype(jnp.float32).reshape(CY, CZ, CX, rhs_count, 2, 2, vectors)
    real_w = weights[:, :, :, :, 0]
    imag_w = weights[:, :, :, :, 1]
    mixer = jnp.stack([jnp.stack([real_w, -imag_w]), jnp.stack([imag_w, real_w])])
    null_view = null_slice.astype(jnp.float32).reshape(4, 2, 2, 6, vectors, CX, 4, CZ, 4, CY, 4)
    result = jnp.einsum("tphgkcxzayb,qpyzcrhk->tqhgrcxzayb", null_view, mixer)
    return result.reshape(4, 2, 12, rhs_count, CX * 4 * CZ * 4 * CY * 4)


def apply_coarse(field, coarse_operator):
    shifted = [field]
    for dimension in range(4):
        shifted.append(jnp.roll(field, -1, dimension))
        shifted.append(jnp.roll(field, 1, dimension))
    stacked = jnp.stack(shifted, axis=1)

    def one_time(pair):
        return jnp.einsum("dyzxij,dyzxrj->yzxri", pair[1].astype(jnp.float32), pair[0].astype(jnp.float32))

    image = lax.map(one_time, (stacked, coarse_operator))
    return image + DIAGONAL_SHIFT * field.astype(jnp.float32)


def reference(fine_vectors, null_vectors, coarse_operator):
    slices = fine_vectors.shape[0] // 4
    fine_blocks = fine_vectors.reshape((slices, 4) + fine_vectors.shape[1:])
    null_blocks = null_vectors.reshape((slices, 4) + null_vectors.shape[1:])
    coarse_sums = lax.map(lambda pair: restrict_slice(pair[0], pair[1]), (fine_blocks, null_blocks))
    coarse_rhs = coarse_sums.astype(jnp.bfloat16)
    target = coarse_rhs.astype(jnp.float32)
    iterate = RELAX_WEIGHT * target
    for sweep_index in range(APPLIES):
        image = apply_coarse(iterate.astype(jnp.bfloat16), coarse_operator)
        iterate = iterate + RELAX_WEIGHT * (target - image)
    coarse_iterate = iterate.astype(jnp.bfloat16)
    fine_parts = lax.map(lambda pair: prolong_slice(pair[0], pair[1]), (coarse_iterate, null_blocks))
    fine_correction = fine_parts.reshape(fine_vectors.shape).astype(jnp.bfloat16)
    return fine_correction, coarse_iterate
```

```python
import functools

import jax
import jax.numpy as jnp
from jax import lax
from jax.experimental import pallas as pl
from jax.experimental.pallas import tpu as pltpu
from jax.sharding import PartitionSpec as P

CZ = 2
APPLIES = 4
RELAX_WEIGHT = 0.3
DIAGONAL_SHIFT = 3.0
LANES = (((1,), (1,)), ((), ()))


def aggregate_ids(shape, coarse_y):
    site = lax.broadcasted_iota(jnp.int32, shape, len(shape) - 1)
    row = 4 * coarse_y
    y = lax.rem(site, row) // 4
    z = lax.rem(site, row * 4 * CZ) // (row * 4)
    return y * CZ + z


def restrict_kernel(coarse_y, fine_ref, null_ref, out_ref, sums):
    step = pl.program_id(0)
    aggregates = coarse_y * CZ
    rhs, sites = fine_ref.shape[3:]
    vectors = null_ref.shape[3]
    ids = aggregate_ids((2 * rhs, sites), coarse_y)
    masks = [(ids == a).astype(jnp.float32).astype(jnp.bfloat16) for a in range(aggregates)]

    @pl.when(step == 0)
    def _():
        sums[...] = jnp.zeros_like(sums)

    for h in range(2):
        left, right = [], []
        for g in range(6):
            c = h * 6 + g
            fine = jnp.concatenate([fine_ref[0, 0, c], fine_ref[0, 1, c]], axis=0)
            left.append(jnp.concatenate([fine * m for m in masks], axis=0))
            right.append(jnp.concatenate([null_ref[0, 0, c], null_ref[0, 1, c]], axis=0))
        sums[h] += lax.dot_general(
            jnp.concatenate(left, axis=1),
            jnp.concatenate(right, axis=1),
            LANES,
            preferred_element_type=jnp.float32,
        )

    @pl.when(step == pl.num_programs(0) - 1)
    def _():
        for a in range(aggregates):
            real, imag = [], []
            for h in range(2):
                top = sums[h, a * 2 * rhs : a * 2 * rhs + rhs]
                low = sums[h, a * 2 * rhs + rhs : (a + 1) * 2 * rhs]
                real.append(top[:, :vectors] + low[:, vectors:])
                imag.append(low[:, :vectors] - top[:, vectors:])
            out_ref[a] = jnp.concatenate(real + imag, axis=1).astype(out_ref.dtype)


def restrict(fine, null):
    times, _, _, rhs, sites = fine.shape
    vectors = null.shape[3]
    coarse_y = sites // (64 * CZ)
    aggregates = coarse_y * CZ
    return pl.pallas_call(
        functools.partial(restrict_kernel, coarse_y),
        grid=(times,),
        in_specs=[
            pl.BlockSpec((1, 2, 12, rhs, sites), lambda t: (t, 0, 0, 0, 0)),
            pl.BlockSpec((1, 2, 12, vectors, sites), lambda t: (t, 0, 0, 0, 0)),
        ],
        out_specs=pl.BlockSpec((aggregates, rhs, 4 * vectors), lambda t: (0, 0, 0)),
        out_shape=jax.ShapeDtypeStruct((aggregates, rhs, 4 * vectors), jnp.bfloat16),
        scratch_shapes=[pltpu.VMEM((2, aggregates * 2 * rhs, 2 * vectors), jnp.float32)],
        name="restrict",
    )(fine, null)


def prolong_kernel(coarse_y, coarse_ref, null_ref, out_ref):
    aggregates = coarse_y * CZ
    rhs, sites = out_ref.shape[3:]
    vectors = null_ref.shape[3]
    ids = aggregate_ids((2 * rhs, sites), coarse_y)
    masks = [ids == a for a in range(aggregates)]
    for h in range(2):
        mixer = []
        for a in range(aggregates):
            weights = coarse_ref[a]
            real = weights[:, h * vectors : (h + 1) * vectors]
            imag = weights[:, (2 + h) * vectors : (3 + h) * vectors]
            mixer.append(jnp.concatenate([real, -imag], axis=1))
            mixer.append(jnp.concatenate([imag, real], axis=1))
        mixer = jnp.concatenate(mixer, axis=0)
        for g in range(6):
            c = h * 6 + g
            null = jnp.concatenate([null_ref[0, 0, c], null_ref[0, 1, c]], axis=0)
            every = jnp.dot(mixer, null, preferred_element_type=jnp.float32)
            result = every[: 2 * rhs]
            for a in range(1, aggregates):
                result = jnp.where(masks[a], every[a * 2 * rhs : (a + 1) * 2 * rhs], result)
            result = result.astype(out_ref.dtype)
            out_ref[0, 0, c] = result[:rhs]
            out_ref[0, 1, c] = result[rhs:]


def prolong(coarse, null):
    aggregates, rhs, _ = coarse.shape
    times, _, _, vectors, sites = null.shape
    return pl.pallas_call(
        functools.partial(prolong_kernel, aggregates // CZ),
        grid=(times,),
        in_specs=[
            pl.BlockSpec(coarse.shape, lambda t: (0, 0, 0)),
            pl.BlockSpec((1, 2, 12, vectors, sites), lambda t: (t, 0, 0, 0, 0)),
        ],
        out_specs=pl.BlockSpec((1, 2, 12, rhs, sites), lambda t: (t, 0, 0, 0, 0)),
        out_shape=jax.ShapeDtypeStruct((times, 2, 12, rhs, sites), jnp.bfloat16),
        name="prolong",
    )(coarse, null)


def padded_2(array, sides, width):
    for axis, dim in sides:
        devices, length = (lax.axis_size(axis), array.shape[dim])
        up = [(i, (i + 1) % devices) for i in range(devices)]
        down = [(j, i) for i, j in up]
        last = lax.slice_in_dim(array, length - width, length, axis=dim)
        initial = lax.slice_in_dim(array, 0, width, axis=dim)
        before = lax.ppermute(last, axis, up)
        after = lax.ppermute(initial, axis, down)
        array = jnp.concatenate([before, array, after], axis=dim)
    return array


def stencil_product(field, shifted, operator_block):
    stacked = jnp.stack(shifted, axis=1)
    image = jnp.einsum(
        "tdyzxij,tdyzxrj->tyzxri", operator_block, stacked, preferred_element_type=jnp.float32
    )
    return image + DIAGONAL_SHIFT * field.astype(jnp.float32)


def apply_whole(field, operator_block):
    padded = padded_2(field, (("zt", 0),), 1)
    shifted = [
        field,
        padded[2:],
        padded[:-2],
        jnp.roll(field, -1, 1),
        jnp.roll(field, 1, 1),
        jnp.roll(field, -1, 2),
        jnp.roll(field, 1, 2),
        jnp.roll(field, -1, 3),
        jnp.roll(field, 1, 3),
    ]
    return stencil_product(field, shifted, operator_block)


def per_device(fine_vectors, null_vectors, coarse_operator):
    position = lax.axis_index("xy")
    sums = restrict(fine_vectors, null_vectors)
    aggregates, rhs, columns = sums.shape
    coarse_rhs = sums.reshape(1, aggregates // CZ, CZ, 1, rhs, columns)
    whole_rhs = lax.all_gather(coarse_rhs, "xy", axis=3, tiled=True)
    target = whole_rhs.astype(jnp.float32)
    iterate = RELAX_WEIGHT * target
    for sweep_index in range(APPLIES):
        image = apply_whole(iterate.astype(jnp.bfloat16), coarse_operator)
        iterate = iterate + RELAX_WEIGHT * (target - image)
    coarse_iterate = iterate.astype(jnp.bfloat16)
    column = lax.dynamic_slice_in_dim(coarse_iterate, position, 1, 3)
    fine_correction = prolong(column.reshape(sums.shape), null_vectors)
    return (fine_correction, coarse_iterate)


def solution(mesh):
    return jax.shard_map(
        per_device,
        mesh=mesh,
        in_specs=(
            P("zt", None, None, None, "xy"),
            P("zt", None, None, None, "xy"),
            P("zt", None, None, None, None, None, None),
        ),
        out_specs=(P("zt", None, None, None, "xy"), P("zt", None, None, None, None, None)),
        check_vma=False,
    )
```

```python
import functools

import jax
import jax.numpy as jnp
from jax import lax
from jax.experimental import pallas as pl
from jax.experimental.pallas import tpu as pltpu
from jax.sharding import PartitionSpec as P

CZ = 2
APPLIES = 4
RELAX_WEIGHT = 0.3
DIAGONAL_SHIFT = 3.0
LANES = (((1,), (1,)), ((), ()))
KERNEL_VMEM = 16 * 1024 * 1024


def aggregate_ids(shape, coarse_y):
    site = lax.broadcasted_iota(jnp.int32, shape, len(shape) - 1)
    row = 4 * coarse_y
    y = lax.rem(site, row) // 4
    z = lax.rem(site, row * 4 * CZ) // (row * 4)
    return y * CZ + z


def restrict_kernel(coarse_y, fine_hbm, null_hbm, operator, out_ref, null_ref, block, fine_ref, loaded):
    aggregates = coarse_y * CZ
    times, _, _, rhs, sites = fine_ref.shape
    vectors = null_ref.shape[3]
    _, odd = time_sides(True)
    loads = []
    for t in range(times):
        loads.append(pltpu.make_async_copy(fine_hbm.at[t], fine_ref.at[t], loaded.at[2 * t]))
        loads.append(pltpu.make_async_copy(null_hbm.at[t], null_ref.at[t], loaded.at[2 * t + 1]))
    loads.append(pltpu.make_async_copy(operator.at[0, odd], block, loaded.at[2 * times]))
    for load in loads:
        load.start()
    ids = aggregate_ids((2 * rhs, sites), coarse_y)
    masks = [(ids == a).astype(jnp.float32).astype(jnp.bfloat16) for a in range(aggregates)]
    sums = [None, None]
    for t in range(times):
        loads[2 * t].wait()
        loads[2 * t + 1].wait()
        for h in range(2):
            left, right = [], []
            for c in range(h * 6, h * 6 + 6):
                fine = jnp.concatenate([fine_ref[t, 0, c], fine_ref[t, 1, c]], axis=0)
                left.append(jnp.concatenate([fine * m for m in masks], axis=0))
                right.append(jnp.concatenate([null_ref[t, 0, c], null_ref[t, 1, c]], axis=0))
            part = lax.dot_general(
                jnp.concatenate(left, axis=1),
                jnp.concatenate(right, axis=1),
                LANES,
                preferred_element_type=jnp.float32,
            )
            sums[h] = part if sums[h] is None else sums[h] + part
    for a in range(aggregates):
        real, imag = [], []
        for h in range(2):
            top = sums[h][a * 2 * rhs : a * 2 * rhs + rhs]
            low = sums[h][a * 2 * rhs + rhs : (a + 1) * 2 * rhs]
            real.append(top[:, :vectors] + low[:, vectors:])
            imag.append(low[:, :vectors] - top[:, vectors:])
        out_ref[a] = jnp.concatenate(real + imag, axis=1).astype(out_ref.dtype)
    loads[-1].wait()


def restrict(fine, null, operator):
    times, _, _, rhs, sites = fine.shape
    coarse_y = sites // (64 * CZ)
    return pl.pallas_call(
        functools.partial(restrict_kernel, coarse_y),
        in_specs=[pl.BlockSpec(memory_space=pl.ANY)] * 3,
        out_specs=[pl.BlockSpec(memory_space=pltpu.VMEM)] * 3,
        out_shape=[
            pltpu.VMEM((coarse_y * CZ, rhs, 4 * null.shape[3]), jnp.bfloat16),
            pltpu.VMEM(null.shape, null.dtype),
            pltpu.VMEM(operator.shape[2:], operator.dtype),
        ],
        scratch_shapes=[pltpu.VMEM(fine.shape, fine.dtype), pltpu.SemaphoreType.DMA((2 * times + 1,))],
        compiler_params=pltpu.CompilerParams(vmem_limit_bytes=KERNEL_VMEM),
        name="restrict",
    )(in_hbm(fine), in_hbm(null), in_hbm(operator))


def prolong_kernel(coarse_y, coarse_ref, null_ref, out_ref, held, done):
    aggregates = coarse_y * CZ
    times, _, _, rhs, sites = held.shape
    vectors = null_ref.shape[3]
    ids = aggregate_ids((2 * rhs, sites), coarse_y)
    masks = [ids == a for a in range(aggregates)]
    mixers = []
    for h in range(2):
        mixer = []
        for a in range(aggregates):
            weights = coarse_ref[a]
            real = weights[:, h * vectors : (h + 1) * vectors]
            imag = weights[:, (2 + h) * vectors : (3 + h) * vectors]
            mixer.append(jnp.concatenate([real, -imag], axis=1))
            mixer.append(jnp.concatenate([imag, real], axis=1))
        mixers.append(jnp.concatenate(mixer, axis=0))
    copies = []
    for t in range(times):
        for c in range(12):
            null = jnp.concatenate([null_ref[t, 0, c], null_ref[t, 1, c]], axis=0)
            every = jnp.dot(mixers[c // 6], null, preferred_element_type=jnp.float32)
            result = every[: 2 * rhs]
            for a in range(1, aggregates):
                result = jnp.where(masks[a], every[a * 2 * rhs : (a + 1) * 2 * rhs], result)
            result = result.astype(held.dtype)
            held[t, 0, c] = result[:rhs]
            held[t, 1, c] = result[rhs:]
        copies.append(pltpu.make_async_copy(held.at[t], out_ref.at[t], done.at[t]))
        copies[-1].start()
    for copy in copies:
        copy.wait()


def prolong(coarse, null):
    aggregates, rhs, _ = coarse.shape
    times, _, _, _, sites = null.shape
    shape = (times, 2, 12, rhs, sites)
    return pl.pallas_call(
        functools.partial(prolong_kernel, aggregates // CZ),
        in_specs=[pl.BlockSpec(memory_space=pltpu.VMEM)] * 2,
        out_specs=pl.BlockSpec(memory_space=pl.ANY),
        out_shape=jax.ShapeDtypeStruct(shape, jnp.bfloat16),
        scratch_shapes=[pltpu.VMEM(shape, jnp.bfloat16), pltpu.SemaphoreType.DMA((times,))],
        compiler_params=pltpu.CompilerParams(vmem_limit_bytes=KERNEL_VMEM),
        name="prolong",
    )(in_vmem(coarse), in_vmem(null))


def time_sides(even_slice):
    parity = lax.rem(lax.axis_index("zt"), 2)
    if not even_slice:
        parity = 1 - parity
    return 1 + parity, 2 - parity


def for_sites(extent, body):
    for y in range(extent[0]):
        for z in range(extent[1]):
            if extent[2] <= 2:
                for x in range(extent[2]):
                    body((y, z, x))
            else:
                lax.fori_loop(0, extent[2], lambda x, c, y=y, z=z: (body((y, z, x)), c)[1], 0)


def around(operator, site, extent):
    found = [(operator[(0, 0) + site], site)]
    for axis in range(3):
        up, down = [
            site[:axis] + (lax.rem(site[axis] + step, extent[axis]) if axis == 2 else (site[axis] + step) % extent[axis],)
            + site[axis + 1 :]
            for step in (1, extent[axis] - 1)
        ]
        ahead, behind = operator[(0, 3 + 2 * axis) + site], operator[(0, 4 + 2 * axis) + site]
        if extent[axis] == 2:
            both = ahead.astype(jnp.float32) + behind.astype(jnp.float32)
            found.append((both.astype(jnp.bfloat16), up))
        else:
            found += [(ahead, up), (behind, down)]
    return found


def products(pairs):
    return lax.dot_general(
        jnp.concatenate([field for _, field in pairs], axis=1),
        jnp.concatenate([block for block, _ in pairs], axis=1),
        LANES,
        preferred_element_type=jnp.float32,
    )


def stencil(operator, site, here, times):
    extent = operator.shape[2:5]
    pairs = [(block, here[near]) for block, near in around(operator, site, extent)]
    pairs += [(operator[(0, d) + site], field[site]) for d, field in times]
    return products(pairs)


def relaxed(value, rounded, target, sums):
    image = sums + DIAGONAL_SHIFT * rounded.astype(jnp.float32)
    return value + RELAX_WEIGHT * (target.astype(jnp.float32) - image)


def gather_kernel(pieces, operator, *refs):
    parts, (rhs_mine, rhs_pair, start_pair, message, part_mine) = refs[: 2 * pieces], refs[2 * pieces :]
    extent = operator.shape[2:5]
    position = lax.axis_index("xy")
    even, _ = time_sides(True)
    for whole, held in ((rhs_mine, parts[:pieces]), (rhs_pair, parts[pieces:])):
        for y in range(extent[0]):
            for z in range(extent[1]):
                for x in range(extent[2]):
                    if pieces == 1:
                        whole[y, z, x] = held[0][x, y * extent[1] + z]
                    else:
                        whole[y, z, lax.rem(position + x, pieces)] = held[x][y * extent[1] + z]

    def begin(site):
        message[(0,) + site] = (RELAX_WEIGHT * rhs_mine[site].astype(jnp.float32)).astype(jnp.bfloat16)
        start_pair[site] = (RELAX_WEIGHT * rhs_pair[site].astype(jnp.float32)).astype(jnp.bfloat16)

    for_sites(extent, begin)
    here = message.at[0]

    def step(site):
        sums = stencil(operator, site, here, [(even, start_pair)])
        value = RELAX_WEIGHT * rhs_mine[site].astype(jnp.float32)
        part = relaxed(value, here[site], rhs_mine[site], sums)
        part_mine[site] = part
        message[(1,) + site] = part.astype(jnp.bfloat16)

    for_sites(extent, step)


def pair_kernel(scaled, operator, rhs_pair, held, here, sent, part_pair, passed=None):
    even, _ = time_sides(False)
    other = sent.at[0]

    def step(site):
        sums = stencil(operator, site, here, [(even, other)])
        if scaled:
            value = RELAX_WEIGHT * rhs_pair[site].astype(jnp.float32)
        else:
            value = held[site]
        part_pair[site] = relaxed(value, here[site], rhs_pair[site], sums)
        if scaled:
            passed[site] = held[site]

    for_sites(operator.shape[2:5], step)


def second_kernel(
    op_mine, op_pair, back_near, back_far, rhs_mine, rhs_pair, sent, start_pair, part_mine, part_pair, near, far,
    message, field_mine, part_next, value_pair, field_pair, one_mine, one_pair, one_near, one_far, x_mine, x_pair,
):
    extent = op_mine.shape[2:5]
    even, odd = time_sides(True)
    pair_even, pair_odd = time_sides(False)

    def first(site):
        value = part_mine[site] - RELAX_WEIGHT * products([(op_mine[(0, odd) + site], near[(0,) + site])])
        x_mine[site] = value
        one_mine[site] = value.astype(jnp.bfloat16)
        value = part_pair[site] - RELAX_WEIGHT * products([(op_pair[(0, pair_odd) + site], far[(0,) + site])])
        x_pair[site] = value
        one_pair[site] = value.astype(jnp.bfloat16)
        value = near[(1,) + site].astype(jnp.float32) - RELAX_WEIGHT * products([(back_near[site], sent[(0,) + site])])
        one_near[site] = value.astype(jnp.bfloat16)
        value = far[(1,) + site].astype(jnp.float32) - RELAX_WEIGHT * products([(back_far[site], start_pair[site])])
        one_far[site] = value.astype(jnp.bfloat16)

    for_sites(extent, first)

    def second(site):
        sums = stencil(op_mine, site, one_mine, [(even, one_pair), (odd, one_near)])
        value = relaxed(x_mine[site], one_mine[site], rhs_mine[site], sums)
        x_mine[site] = value
        message[(0,) + site] = value.astype(jnp.bfloat16)
        field_mine[site] = value.astype(jnp.bfloat16)
        sums = stencil(op_pair, site, one_pair, [(pair_even, one_mine), (pair_odd, one_far)])
        value = relaxed(x_pair[site], one_pair[site], rhs_pair[site], sums)
        value_pair[site] = value
        field_pair[site] = value.astype(jnp.bfloat16)

    for_sites(extent, second)
    here = message.at[0]

    def third(site):
        sums = stencil(op_mine, site, here, [(even, field_pair)])
        part = relaxed(x_mine[site], here[site], rhs_mine[site], sums)
        part_next[site] = part
        message[(1,) + site] = part.astype(jnp.bfloat16)

    for_sites(extent, third)


def last_kernel(
    op_mine, op_pair, back_near, rhs_mine, sent, part_mine, part_pair, near, far,
    result, column, one_mine, one_pair, one_near, x_mine,
):
    extent = op_mine.shape[2:5]
    even, odd = time_sides(True)
    _, pair_odd = time_sides(False)

    def first(site):
        value = part_mine[site] - RELAX_WEIGHT * products([(op_mine[(0, odd) + site], near[(0,) + site])])
        x_mine[site] = value
        one_mine[site] = value.astype(jnp.bfloat16)
        value = part_pair[site] - RELAX_WEIGHT * products([(op_pair[(0, pair_odd) + site], far[site])])
        one_pair[site] = value.astype(jnp.bfloat16)
        value = near[(1,) + site].astype(jnp.float32) - RELAX_WEIGHT * products([(back_near[site], sent[(0,) + site])])
        one_near[site] = value.astype(jnp.bfloat16)

    for_sites(extent, first)

    def second(site):
        sums = stencil(op_mine, site, one_mine, [(even, one_pair), (odd, one_near)])
        value = relaxed(x_mine[site], one_mine[site], rhs_mine[site], sums)
        result[(0,) + site] = value.astype(jnp.bfloat16)

    for_sites(extent, second)
    position = lax.axis_index("xy")
    for y in range(extent[0]):
        for z in range(extent[1]):
            column[y * extent[1] + z] = result[0, y, z, position]


def in_hbm(array):
    return pltpu.with_memory_space_constraint(array, pltpu.HBM)


def in_vmem(array):
    return pltpu.with_memory_space_constraint(array, pltpu.VMEM)


def kernel_call(kernel, name, outs, scratch, *operands):
    return pl.pallas_call(
        kernel,
        in_specs=[pl.BlockSpec(memory_space=pltpu.VMEM)] * len(operands),
        out_specs=[pl.BlockSpec(memory_space=pltpu.VMEM)] * len(outs),
        out_shape=[pltpu.VMEM(shape, dtype) for shape, dtype in outs],
        scratch_shapes=[pltpu.VMEM(shape, dtype) for shape, dtype in scratch],
        compiler_params=pltpu.CompilerParams(vmem_limit_bytes=KERNEL_VMEM),
        name=name,
    )(*[in_vmem(operand) for operand in operands])


def exchange_plan():
    slices, columns = lax.axis_size("zt"), lax.axis_size("xy")
    other = [i ^ 1 for i in range(slices)]
    across = [(i + 1 if i % 2 else i - 1) % slices for i in range(slices)]

    def permutation(target, turn=0):
        return [
            (i * columns + j, target[i] * columns + (j + turn) % columns) for i in range(slices) for j in range(columns)
        ]

    def send(array, target, turn=0):
        return lax.ppermute(array, ("zt", "xy"), permutation(target, turn))

    far = [other[across[i]] for i in range(slices)]
    return send, list(range(slices)), other, across, far


def per_device(fine_vectors, null_vectors, coarse_operator):
    send, same, other, across, far = exchange_plan()
    columns = lax.axis_size("xy")
    extent = coarse_operator.shape[2:5]
    bf16, f32 = jnp.bfloat16, jnp.float32
    own, null_kept, block = restrict(fine_vectors, null_vectors, coarse_operator)
    full = extent + own.shape[1:]
    if columns == 2:
        parts = [own, send(own, same, 1), send(own, other), send(own, other, 1)]
    else:
        every = lax.all_gather(own, "xy")
        parts = [every, send(every, other)]
    back_near = send(block, across)
    op_pair = send(coarse_operator, other)
    rhs_mine, rhs_pair, start_pair, sent, part_mine = kernel_call(
        functools.partial(gather_kernel, len(parts) // 2),
        "gather",
        [(full, bf16), (full, bf16), (full, bf16), ((2,) + full, bf16), (full, f32)],
        [],
        coarse_operator,
        *parts,
    )
    near_message, far_message = send(sent, across), send(sent, far)
    part_pair, back_far = kernel_call(
        functools.partial(pair_kernel, True), "pair_one", [(full, f32), (block.shape, bf16)], [],
        op_pair, rhs_pair, back_near, start_pair, sent,
    )
    back_far = send(back_far, other)
    sent_next, field_mine, part_mine, value_pair, field_pair = kernel_call(
        second_kernel,
        "second",
        [((2,) + full, bf16), (full, bf16), (full, f32), (full, f32), (full, bf16)],
        [(full, bf16)] * 4 + [(full, f32)] * 2,
        coarse_operator, op_pair, back_near, back_far, rhs_mine, rhs_pair, sent, start_pair, part_mine, part_pair,
        near_message, far_message,
    )
    near_message, far_field = send(sent_next, across), send(field_mine, far)
    (part_pair,) = kernel_call(
        functools.partial(pair_kernel, False), "pair_two", [(full, f32)], [],
        op_pair, rhs_pair, value_pair, field_pair, sent_next,
    )
    coarse_iterate, column = kernel_call(
        last_kernel,
        "last",
        [((1,) + full, bf16), (own.shape, bf16)],
        [(full, bf16)] * 3 + [(full, f32)],
        coarse_operator, op_pair, back_near, rhs_mine, sent_next, part_mine, part_pair, near_message, far_field,
    )
    return (prolong(column, null_kept), coarse_iterate)


def solution(mesh):
    return jax.shard_map(
        per_device,
        mesh=mesh,
        in_specs=(
            P("zt", None, None, None, "xy"),
            P("zt", None, None, None, "xy"),
            P("zt", None, None, None, None, None, None),
        ),
        out_specs=(P("zt", None, None, None, "xy"), P("zt", None, None, None, None, None)),
        check_vma=False,
    )
```

```python
import functools

import jax
import jax.numpy as jnp
from jax import lax
from jax.experimental import pallas as pl
from jax.experimental.pallas import tpu as pltpu
from jax.sharding import PartitionSpec as P

CZ = 2
APPLIES = 4
RELAX_WEIGHT = 0.3
DIAGONAL_SHIFT = 3.0
LANES = (((1,), (1,)), ((), ()))
KERNEL_VMEM = 16 * 1024 * 1024
GATHER_FLOPS = 10**10


def aggregate_ids(shape, coarse_y):
    site = lax.broadcasted_iota(jnp.int32, shape, len(shape) - 1)
    row = 4 * coarse_y
    y = lax.rem(site, row) // 4
    z = lax.rem(site, row * 4 * CZ) // (row * 4)
    return y * CZ + z


def restrict_kernel(coarse_y, fine_hbm, null_hbm, operator_hbm, out_ref, null_ref, operator, block, fine_ref, loaded):
    aggregates = coarse_y * CZ
    times, _, _, rhs, sites = fine_ref.shape
    vectors = null_ref.shape[3]
    _, odd = time_sides(True)
    loads = []
    for t in range(times):
        loads.append(pltpu.make_async_copy(fine_hbm.at[t], fine_ref.at[t], loaded.at[2 * t]))
        loads.append(pltpu.make_async_copy(null_hbm.at[t], null_ref.at[t], loaded.at[2 * t + 1]))
    loads.append(pltpu.make_async_copy(operator_hbm.at[0, odd], block, loaded.at[2 * times]))
    loads.append(pltpu.make_async_copy(operator_hbm, operator, loaded.at[2 * times + 1]))
    for load in loads:
        load.start()
    ids = aggregate_ids((2 * rhs, sites), coarse_y)
    masks = [(ids == a).astype(jnp.float32).astype(jnp.bfloat16) for a in range(aggregates)]
    sums = [None, None]
    for t in range(times):
        loads[2 * t].wait()
        loads[2 * t + 1].wait()
        for h in range(2):
            left, right = [], []
            for c in range(h * 6, h * 6 + 6):
                fine = jnp.concatenate([fine_ref[t, 0, c], fine_ref[t, 1, c]], axis=0)
                left.append(jnp.concatenate([fine * m for m in masks], axis=0))
                right.append(jnp.concatenate([null_ref[t, 0, c], null_ref[t, 1, c]], axis=0))
            part = lax.dot_general(
                jnp.concatenate(left, axis=1),
                jnp.concatenate(right, axis=1),
                LANES,
                preferred_element_type=jnp.float32,
            )
            sums[h] = part if sums[h] is None else sums[h] + part
    for a in range(aggregates):
        real, imag = [], []
        for h in range(2):
            top = sums[h][a * 2 * rhs : a * 2 * rhs + rhs]
            low = sums[h][a * 2 * rhs + rhs : (a + 1) * 2 * rhs]
            real.append(top[:, :vectors] + low[:, vectors:])
            imag.append(low[:, :vectors] - top[:, vectors:])
        out_ref[a] = jnp.concatenate(real + imag, axis=1).astype(out_ref.dtype)
    loads[-2].wait()
    loads[-1].wait()


def restrict(fine, null, operator):
    times, _, _, rhs, sites = fine.shape
    coarse_y = sites // (64 * CZ)
    return pl.pallas_call(
        functools.partial(restrict_kernel, coarse_y),
        in_specs=[pl.BlockSpec(memory_space=pl.ANY)] * 3,
        out_specs=[pl.BlockSpec(memory_space=pltpu.VMEM)] * 4,
        out_shape=[
            pltpu.VMEM((coarse_y * CZ, rhs, 4 * null.shape[3]), jnp.bfloat16),
            pltpu.VMEM(null.shape, null.dtype),
            pltpu.VMEM(operator.shape, operator.dtype),
            pltpu.VMEM(operator.shape[2:], operator.dtype),
        ],
        scratch_shapes=[pltpu.VMEM(fine.shape, fine.dtype), pltpu.SemaphoreType.DMA((2 * times + 2,))],
        compiler_params=pltpu.CompilerParams(vmem_limit_bytes=KERNEL_VMEM),
        name="restrict",
    )(in_hbm(fine), in_hbm(null), in_hbm(operator))


def prolong(column, null_ref, out_ref, held, done):
    aggregates = len(column)
    coarse_y = aggregates // CZ
    times, _, _, rhs, sites = held.shape
    vectors = null_ref.shape[3]
    ids = aggregate_ids((2 * rhs, sites), coarse_y)
    masks = [ids == a for a in range(aggregates)]
    mixers = []
    for h in range(2):
        mixer = []
        for a in range(aggregates):
            weights = column[a]
            real = weights[:, h * vectors : (h + 1) * vectors]
            imag = weights[:, (2 + h) * vectors : (3 + h) * vectors]
            mixer.append(jnp.concatenate([real, -imag], axis=1))
            mixer.append(jnp.concatenate([imag, real], axis=1))
        mixers.append(jnp.concatenate(mixer, axis=0))
    copies = []
    for t in range(times):
        for c in range(12):
            null = jnp.concatenate([null_ref[t, 0, c], null_ref[t, 1, c]], axis=0)
            every = jnp.dot(mixers[c // 6], null, preferred_element_type=jnp.float32)
            result = every[: 2 * rhs]
            for a in range(1, aggregates):
                result = jnp.where(masks[a], every[a * 2 * rhs : (a + 1) * 2 * rhs], result)
            result = result.astype(held.dtype)
            held[t, 0, c] = result[:rhs]
            held[t, 1, c] = result[rhs:]
        copies.append(pltpu.make_async_copy(held.at[t], out_ref.at[t], done.at[t]))
        copies[-1].start()
    for copy in copies:
        copy.wait()


def time_sides(even_slice):
    parity = lax.rem(lax.axis_index("zt"), 2)
    if not even_slice:
        parity = 1 - parity
    return 1 + parity, 2 - parity


def for_sites(extent, body):
    for y in range(extent[0]):
        for z in range(extent[1]):
            if extent[2] <= 2:
                for x in range(extent[2]):
                    body((y, z, x))
            else:
                lax.fori_loop(0, extent[2], lambda x, c, y=y, z=z: (body((y, z, x)), c)[1], 0)


def around(operator, site, extent):
    found = [(operator[(0, 0) + site], site)]
    for axis in range(3):
        up, down = [
            site[:axis] + (lax.rem(site[axis] + step, extent[axis]) if axis == 2 else (site[axis] + step) % extent[axis],)
            + site[axis + 1 :]
            for step in (1, extent[axis] - 1)
        ]
        ahead, behind = operator[(0, 3 + 2 * axis) + site], operator[(0, 4 + 2 * axis) + site]
        if extent[axis] == 2:
            both = ahead.astype(jnp.float32) + behind.astype(jnp.float32)
            found.append((both.astype(jnp.bfloat16), up))
        else:
            found += [(ahead, up), (behind, down)]
    return found


def products(pairs):
    return lax.dot_general(
        jnp.concatenate([field for _, field in pairs], axis=1),
        jnp.concatenate([block for block, _ in pairs], axis=1),
        LANES,
        preferred_element_type=jnp.float32,
    )


def stencil(operator, site, here, times):
    extent = operator.shape[2:5]
    pairs = [(block, here[near]) for block, near in around(operator, site, extent)]
    pairs += [(operator[(0, d) + site], field[site]) for d, field in times]
    return products(pairs)


def relaxed(value, rounded, target, sums):
    image = sums + DIAGONAL_SHIFT * rounded.astype(jnp.float32)
    return value + RELAX_WEIGHT * (target.astype(jnp.float32) - image)


def gather_kernel(pieces, operator, *refs):
    parts, (rhs_mine, rhs_pair, start_mine, start_pair, message, part_mine) = refs[: 2 * pieces], refs[2 * pieces :]
    extent = operator.shape[2:5]
    position = lax.axis_index("xy")
    even, _ = time_sides(True)
    for whole, held in ((rhs_mine, parts[:pieces]), (rhs_pair, parts[pieces:])):
        for y in range(extent[0]):
            for z in range(extent[1]):
                for x in range(extent[2]):
                    if pieces == 1:
                        whole[y, z, x] = held[0][x, y * extent[1] + z]
                    else:
                        whole[y, z, lax.rem(position + x, pieces)] = held[x][y * extent[1] + z]

    def begin(site):
        start_mine[site] = (RELAX_WEIGHT * rhs_mine[site].astype(jnp.float32)).astype(jnp.bfloat16)
        message[(0,) + site] = start_mine[site]
        start_pair[site] = (RELAX_WEIGHT * rhs_pair[site].astype(jnp.float32)).astype(jnp.bfloat16)

    for_sites(extent, begin)
    here = start_mine

    def step(site):
        sums = stencil(operator, site, here, [(even, start_pair)])
        value = RELAX_WEIGHT * rhs_mine[site].astype(jnp.float32)
        part = relaxed(value, here[site], rhs_mine[site], sums)
        part_mine[site] = part
        message[(1,) + site] = part.astype(jnp.bfloat16)

    for_sites(extent, step)


def pair_kernel(scaled, operator, rhs_pair, here, other, part_pair):
    even, _ = time_sides(False)

    def step(site):
        sums = stencil(operator, site, here, [(even, other)])
        if scaled:
            value = RELAX_WEIGHT * rhs_pair[site].astype(jnp.float32)
        else:
            value = here[site].astype(jnp.float32)
        part_pair[site] = relaxed(value, here[site], rhs_pair[site], sums)

    for_sites(operator.shape[2:5], step)


def second_kernel(
    op_mine, op_pair, back_near, rhs_mine, sent, part_mine, part_pair, near, far,
    field_mine, value_mine, one_mine, one_pair, one_near, x_mine,
):
    halfway(op_mine, op_pair, back_near, sent, part_mine, part_pair, near, far, one_mine, one_pair, one_near, x_mine)

    def second(site):
        value = second_step(op_mine, rhs_mine, one_mine, one_pair, one_near, x_mine, site)
        value_mine[site] = value
        field_mine[site] = value.astype(jnp.bfloat16)

    for_sites(op_mine.shape[2:5], second)


def halfway(op_mine, op_pair, back_near, sent, part_mine, part_pair, near, far, one_mine, one_pair, one_near, x_mine):
    _, odd = time_sides(True)
    _, pair_odd = time_sides(False)

    def first(site):
        value = part_mine[site] - RELAX_WEIGHT * products([(op_mine[(0, odd) + site], near[(0,) + site])])
        x_mine[site] = value
        one_mine[site] = value.astype(jnp.bfloat16)
        value = part_pair[site] - RELAX_WEIGHT * products([(op_pair[(0, pair_odd) + site], far[site])])
        one_pair[site] = value.astype(jnp.bfloat16)
        value = near[(1,) + site].astype(jnp.float32) - RELAX_WEIGHT * products([(back_near[site], sent[(0,) + site])])
        one_near[site] = value.astype(jnp.bfloat16)

    for_sites(op_mine.shape[2:5], first)


def second_step(op_mine, rhs_mine, one_mine, one_pair, one_near, x_mine, site):
    even, odd = time_sides(True)
    sums = stencil(op_mine, site, one_mine, [(even, one_pair), (odd, one_near)])
    return relaxed(x_mine[site], one_mine[site], rhs_mine[site], sums)


def third_kernel(op_mine, rhs_mine, field_mine, value_mine, field_pair, message, part_next):
    even, _ = time_sides(True)

    def third(site):
        sums = stencil(op_mine, site, field_mine, [(even, field_pair)])
        part = relaxed(value_mine[site], field_mine[site], rhs_mine[site], sums)
        part_next[site] = part
        message[(0,) + site] = field_mine[site]
        message[(1,) + site] = part.astype(jnp.bfloat16)

    for_sites(op_mine.shape[2:5], third)


def last_kernel(
    op_mine, op_pair, back_near, rhs_mine, sent, part_mine, part_pair, near, far, null,
    fine_out, coarse_out, one_mine, one_pair, one_near, x_mine, result, held, done,
):
    extent = op_mine.shape[2:5]
    halfway(op_mine, op_pair, back_near, sent, part_mine, part_pair, near, far, one_mine, one_pair, one_near, x_mine)

    def second(site):
        value = second_step(op_mine, rhs_mine, one_mine, one_pair, one_near, x_mine, site)
        result[(0,) + site] = value.astype(jnp.bfloat16)

    for_sites(extent, second)
    times = held.shape[0]
    copy = pltpu.make_async_copy(result, coarse_out, done.at[times])
    copy.start()
    position = lax.axis_index("xy")
    column = [result[0, y, z, position] for y in range(extent[0]) for z in range(extent[1])]
    prolong(column, null, fine_out, held, done)
    copy.wait()


def last(shape, *operands):
    full, times = operands[5].shape, shape[0]
    return pl.pallas_call(
        last_kernel,
        in_specs=[pl.BlockSpec(memory_space=pltpu.VMEM)] * len(operands),
        out_specs=[pl.BlockSpec(memory_space=pl.ANY)] * 2,
        out_shape=[
            jax.ShapeDtypeStruct(shape, jnp.bfloat16),
            jax.ShapeDtypeStruct((1,) + full, jnp.bfloat16),
        ],
        scratch_shapes=[pltpu.VMEM(full, jnp.bfloat16)] * 3
        + [
            pltpu.VMEM(full, jnp.float32),
            pltpu.VMEM((1,) + full, jnp.bfloat16),
            pltpu.VMEM(shape, jnp.bfloat16),
            pltpu.SemaphoreType.DMA((times + 1,)),
        ],
        compiler_params=pltpu.CompilerParams(vmem_limit_bytes=KERNEL_VMEM),
        name="last",
    )(*[in_vmem(operand) for operand in operands])


def in_hbm(array):
    return pltpu.with_memory_space_constraint(array, pltpu.HBM)


def in_vmem(array):
    return pltpu.with_memory_space_constraint(array, pltpu.VMEM)


def kernel_call(kernel, name, outs, scratch, *operands, flops=0):
    return pl.pallas_call(
        kernel,
        in_specs=[pl.BlockSpec(memory_space=pltpu.VMEM)] * len(operands),
        out_specs=[pl.BlockSpec(memory_space=pltpu.VMEM)] * len(outs),
        out_shape=[pltpu.VMEM(shape, dtype) for shape, dtype in outs],
        scratch_shapes=[pltpu.VMEM(shape, dtype) for shape, dtype in scratch],
        compiler_params=pltpu.CompilerParams(vmem_limit_bytes=KERNEL_VMEM),
        cost_estimate=pl.CostEstimate(flops=flops, bytes_accessed=0, transcendentals=0) if flops else None,
        name=name,
    )(*[in_vmem(operand) for operand in operands])


def exchange_plan():
    slices, columns = lax.axis_size("zt"), lax.axis_size("xy")
    other = [i ^ 1 for i in range(slices)]
    across = [(i + 1 if i % 2 else i - 1) % slices for i in range(slices)]

    def permutation(target, turn=0):
        return [
            (i * columns + j, target[i] * columns + (j + turn) % columns) for i in range(slices) for j in range(columns)
        ]

    def send(array, target, turn=0):
        return lax.ppermute(array, ("zt", "xy"), permutation(target, turn))

    far = [other[across[i]] for i in range(slices)]
    return send, list(range(slices)), other, across, far


def per_device(fine_vectors, null_vectors, coarse_operator):
    send, same, other, across, far = exchange_plan()
    columns = lax.axis_size("xy")
    extent = coarse_operator.shape[2:5]
    bf16, f32 = jnp.bfloat16, jnp.float32
    own, null_kept, operator, block = restrict(fine_vectors, null_vectors, coarse_operator)
    full = extent + own.shape[1:]
    if columns == 2:
        parts = [own, send(own, same, 1), send(own, other), send(own, other, 1)]
    else:
        every = lax.all_gather(own, "xy")
        parts = [every, send(every, other)]
    back_near = send(block, across)
    op_pair = send(operator, other)
    rhs_mine, rhs_pair, start_mine, start_pair, sent, part_mine = kernel_call(
        functools.partial(gather_kernel, len(parts) // 2),
        "gather",
        [(full, bf16)] * 4 + [((2,) + full, bf16), (full, f32)],
        [],
        operator,
        *parts,
        flops=GATHER_FLOPS,
    )
    near_message, far_field = send(sent, across), send(start_mine, far)
    (part_pair,) = kernel_call(
        functools.partial(pair_kernel, True), "pair_one", [(full, f32)], [],
        op_pair, rhs_pair, start_pair, start_mine,
    )
    field_mine, value_mine = kernel_call(
        second_kernel,
        "second",
        [(full, bf16), (full, f32)],
        [(full, bf16)] * 3 + [(full, f32)],
        operator, op_pair, back_near, rhs_mine, sent, part_mine, part_pair, near_message, far_field,
    )
    field_pair = send(field_mine, other)
    sent, part_mine = kernel_call(
        third_kernel, "third", [((2,) + full, bf16), (full, f32)], [],
        operator, rhs_mine, field_mine, value_mine, field_pair,
    )
    near_message, far_field = send(sent, across), send(field_mine, far)
    (part_pair,) = kernel_call(
        functools.partial(pair_kernel, False), "pair_two", [(full, f32)], [],
        op_pair, rhs_pair, field_pair, field_mine,
    )
    fine_correction, coarse_iterate = last(
        fine_vectors.shape,
        operator, op_pair, back_near, rhs_mine, sent, part_mine, part_pair, near_message, far_field, null_kept,
    )
    return (fine_correction, coarse_iterate)


def solution(mesh):
    return jax.shard_map(
        per_device,
        mesh=mesh,
        in_specs=(
            P("zt", None, None, None, "xy"),
            P("zt", None, None, None, "xy"),
            P("zt", None, None, None, None, None, None),
        ),
        out_specs=(P("zt", None, None, None, "xy"), P("zt", None, None, None, None, None)),
        check_vma=False,
    )
```

```python
import functools

import jax
import jax.numpy as jnp
from jax import lax
from jax.experimental import pallas as pl
from jax.experimental.pallas import tpu as pltpu
from jax.sharding import PartitionSpec as P

CZ = 2
APPLIES = 4
RELAX_WEIGHT = 0.3
DIAGONAL_SHIFT = 3.0
LANES = (((1,), (1,)), ((), ()))
KERNEL_VMEM = 16 * 1024 * 1024
GATHER_FLOPS = 10**10


def aggregate_ids(shape, coarse_y):
    site = lax.broadcasted_iota(jnp.int32, shape, len(shape) - 1)
    row = 4 * coarse_y
    y = lax.rem(site, row) // 4
    z = lax.rem(site, row * 4 * CZ) // (row * 4)
    return y * CZ + z


def restrict_kernel(coarse_y, fine_hbm, null_hbm, operator_hbm, out_ref, null_ref, operator, block, fine_ref, loaded):
    aggregates = coarse_y * CZ
    times, _, _, rhs, sites = fine_ref.shape
    vectors = null_ref.shape[3]
    _, odd = time_sides(True)
    loads = []
    for t in range(times):
        loads.append(pltpu.make_async_copy(fine_hbm.at[t], fine_ref.at[t], loaded.at[2 * t]))
        loads.append(pltpu.make_async_copy(null_hbm.at[t], null_ref.at[t], loaded.at[2 * t + 1]))
    loads.append(pltpu.make_async_copy(operator_hbm.at[0, odd], block, loaded.at[2 * times]))
    loads.append(pltpu.make_async_copy(operator_hbm, operator, loaded.at[2 * times + 1]))
    for load in loads:
        load.start()
    ids = aggregate_ids((2 * rhs, sites), coarse_y)
    masks = [(ids == a).astype(jnp.float32).astype(jnp.bfloat16) for a in range(aggregates)]
    sums = [None, None]
    for t in range(times):
        loads[2 * t].wait()
        loads[2 * t + 1].wait()
        for h in range(2):
            left, right = [], []
            for c in range(h * 6, h * 6 + 6):
                fine = jnp.concatenate([fine_ref[t, 0, c], fine_ref[t, 1, c]], axis=0)
                left.append(jnp.concatenate([fine * m for m in masks], axis=0))
                right.append(jnp.concatenate([null_ref[t, 0, c], null_ref[t, 1, c]], axis=0))
            part = lax.dot_general(
                jnp.concatenate(left, axis=1),
                jnp.concatenate(right, axis=1),
                LANES,
                preferred_element_type=jnp.float32,
            )
            sums[h] = part if sums[h] is None else sums[h] + part
    for a in range(aggregates):
        real, imag = [], []
        for h in range(2):
            top = sums[h][a * 2 * rhs : a * 2 * rhs + rhs]
            low = sums[h][a * 2 * rhs + rhs : (a + 1) * 2 * rhs]
            real.append(top[:, :vectors] + low[:, vectors:])
            imag.append(low[:, :vectors] - top[:, vectors:])
        out_ref[a] = jnp.concatenate(real + imag, axis=1).astype(out_ref.dtype)
    loads[-2].wait()
    loads[-1].wait()


def restrict(fine, null, operator):
    times, _, _, rhs, sites = fine.shape
    coarse_y = sites // (64 * CZ)
    return pl.pallas_call(
        functools.partial(restrict_kernel, coarse_y),
        in_specs=[pl.BlockSpec(memory_space=pl.ANY)] * 3,
        out_specs=[pl.BlockSpec(memory_space=pltpu.VMEM)] * 4,
        out_shape=[
            pltpu.VMEM((coarse_y * CZ, rhs, 4 * null.shape[3]), jnp.bfloat16),
            pltpu.VMEM(null.shape, null.dtype),
            pltpu.VMEM(operator.shape, operator.dtype),
            pltpu.VMEM(operator.shape[2:], operator.dtype),
        ],
        scratch_shapes=[pltpu.VMEM(fine.shape, fine.dtype), pltpu.SemaphoreType.DMA((2 * times + 2,))],
        compiler_params=pltpu.CompilerParams(vmem_limit_bytes=KERNEL_VMEM),
        name="restrict",
    )(in_hbm(fine), in_hbm(null), in_hbm(operator))


def prolong(column, null_ref, out_ref, held, done):
    coarse_y = len(column) // CZ
    times, _, _, rhs, sites = held.shape
    vectors = null_ref.shape[3]
    ids = aggregate_ids((2 * vectors, sites), coarse_y)
    masks = [(lax.rem(ids, CZ) == z).astype(jnp.float32).astype(jnp.bfloat16) for z in range(CZ)]
    rows = aggregate_ids((2 * rhs, sites), coarse_y) // CZ
    mixers = []
    for h in range(2):
        mixer = []
        for y in range(coarse_y):
            real = [column[y * CZ + z][:, h * vectors : (h + 1) * vectors] for z in range(CZ)]
            imag = [column[y * CZ + z][:, (2 + h) * vectors : (3 + h) * vectors] for z in range(CZ)]
            mixer.append(jnp.concatenate([part for z in range(CZ) for part in (real[z], -imag[z])], axis=1))
            mixer.append(jnp.concatenate([part for z in range(CZ) for part in (imag[z], real[z])], axis=1))
        mixers.append(jnp.concatenate(mixer, axis=0))
    copies = []
    for t in range(times):
        for c in range(12):
            null = jnp.concatenate([null_ref[t, 0, c], null_ref[t, 1, c]], axis=0)
            null = jnp.concatenate([null * mask for mask in masks], axis=0)
            every = jnp.dot(mixers[c // 6], null, preferred_element_type=jnp.float32)
            result = every[: 2 * rhs]
            for y in range(1, coarse_y):
                result = jnp.where(rows == y, every[y * 2 * rhs : (y + 1) * 2 * rhs], result)
            result = result.astype(held.dtype)
            held[t, 0, c] = result[:rhs]
            held[t, 1, c] = result[rhs:]
        copies.append(pltpu.make_async_copy(held.at[t], out_ref.at[t], done.at[t]))
        copies[-1].start()
    for copy in copies:
        copy.wait()


def time_sides(even_slice):
    parity = lax.rem(lax.axis_index("zt"), 2)
    if not even_slice:
        parity = 1 - parity
    return 1 + parity, 2 - parity


def for_sites(extent, body):
    for y in range(extent[0]):
        for z in range(extent[1]):
            if extent[2] <= 2:
                for x in range(extent[2]):
                    body((y, z, x))
            else:
                lax.fori_loop(0, extent[2], lambda x, c, y=y, z=z: (body((y, z, x)), c)[1], 0)


def nearby(site, extent):
    found = [site]
    for axis in range(3):
        for step in [1] if extent[axis] == 2 else [1, extent[axis] - 1]:
            moved = site[axis] + step
            moved = lax.rem(moved, extent[axis]) if axis == 2 else moved % extent[axis]
            found.append(site[:axis] + (moved,) + site[axis + 1 :])
    return found


def around(operator, site, extent):
    blocks = [operator[(0, 0) + site]]
    for axis in range(3):
        ahead, behind = operator[(0, 3 + 2 * axis) + site], operator[(0, 4 + 2 * axis) + site]
        if extent[axis] == 2:
            both = ahead.astype(jnp.float32) + behind.astype(jnp.float32)
            blocks.append(both.astype(jnp.bfloat16))
        else:
            blocks += [ahead, behind]
    return list(zip(blocks, nearby(site, extent)))


def products(pairs):
    return lax.dot_general(
        jnp.concatenate([field for _, field in pairs], axis=1),
        jnp.concatenate([block for block, _ in pairs], axis=1),
        LANES,
        preferred_element_type=jnp.float32,
    )


def packed(operator, site, times):
    blocks = [block for block, _ in around(operator, site, operator.shape[2:5])]
    blocks += [operator[(0, d) + site] for d in times]
    return jnp.concatenate([block.T for block in blocks], axis=0)


def packed_stencil(weights, site, here, times):
    extent = weights.shape[:3]
    fields = [here[near] for near in nearby(site, extent)] + [field[site] for field in times]
    depth = len(fields) * weights.shape[4]
    return jnp.dot(jnp.concatenate(fields, axis=1), weights[site][:depth], preferred_element_type=jnp.float32)


def stencil(operator, site, here, times):
    extent = operator.shape[2:5]
    pairs = [(block, here[near]) for block, near in around(operator, site, extent)]
    pairs += [(operator[(0, d) + site], field[site]) for d, field in times]
    return products(pairs)


def relaxed(value, rounded, target, sums):
    image = sums + DIAGONAL_SHIFT * rounded.astype(jnp.float32)
    return value + RELAX_WEIGHT * (target.astype(jnp.float32) - image)


def gather_kernel(pieces, operator, *refs):
    parts, (rhs_mine, rhs_pair, start_mine, start_pair, message, part_mine) = refs[: 2 * pieces], refs[2 * pieces :]
    extent = operator.shape[2:5]
    position = lax.axis_index("xy")
    even, _ = time_sides(True)
    for whole, held in ((rhs_mine, parts[:pieces]), (rhs_pair, parts[pieces:])):
        for y in range(extent[0]):
            for z in range(extent[1]):
                for x in range(extent[2]):
                    if pieces == 1:
                        whole[y, z, x] = held[0][x, y * extent[1] + z]
                    else:
                        whole[y, z, lax.rem(position + x, pieces)] = held[x][y * extent[1] + z]

    def begin(site):
        start_mine[site] = (RELAX_WEIGHT * rhs_mine[site].astype(jnp.float32)).astype(jnp.bfloat16)
        message[(0,) + site] = start_mine[site]
        start_pair[site] = (RELAX_WEIGHT * rhs_pair[site].astype(jnp.float32)).astype(jnp.bfloat16)

    for_sites(extent, begin)
    here = start_mine

    def step(site):
        sums = stencil(operator, site, here, [(even, start_pair)])
        value = RELAX_WEIGHT * rhs_mine[site].astype(jnp.float32)
        part = relaxed(value, here[site], rhs_mine[site], sums)
        part_mine[site] = part
        message[(1,) + site] = part.astype(jnp.bfloat16)

    for_sites(extent, step)


def first_pair_kernel(op_mine, op_pair, rhs_pair, here, other, part_pair, packed_mine, packed_pair):
    sides, pair_sides = time_sides(True), time_sides(False)

    def step(site):
        packed_mine[site] = packed(op_mine, site, sides)
        packed_pair[site] = packed(op_pair, site, pair_sides)
        sums = packed_stencil(packed_pair, site, here, [other])
        value = RELAX_WEIGHT * rhs_pair[site].astype(jnp.float32)
        part_pair[site] = relaxed(value, here[site], rhs_pair[site], sums)

    for_sites(op_mine.shape[2:5], step)


def second_pair_kernel(packed_pair, rhs_pair, here, other, part_pair):
    def step(site):
        sums = packed_stencil(packed_pair, site, here, [other])
        part_pair[site] = relaxed(here[site].astype(jnp.float32), here[site], rhs_pair[site], sums)

    for_sites(packed_pair.shape[:3], step)


def second_kernel(
    op_mine, op_pair, back_near, rhs_mine, sent, part_mine, part_pair, near, far,
    field_mine, value_mine, one_mine, one_pair, one_near, x_mine,
):
    halfway(op_mine, op_pair, back_near, sent, part_mine, part_pair, near, far, one_mine, one_pair, one_near, x_mine)

    def second(site):
        value = second_step(op_mine, rhs_mine, one_mine, one_pair, one_near, x_mine, site)
        value_mine[site] = value
        field_mine[site] = value.astype(jnp.bfloat16)

    for_sites(op_mine.shape[:3], second)


def halfway(op_mine, op_pair, back_near, sent, part_mine, part_pair, near, far, one_mine, one_pair, one_near, x_mine):
    depth, columns = op_mine.shape[3:]
    side = slice(depth - columns, depth)

    def first(site):
        value = part_mine[site] - RELAX_WEIGHT * product(near[(0,) + site], op_mine[site][side])
        x_mine[site] = value
        one_mine[site] = value.astype(jnp.bfloat16)
        value = part_pair[site] - RELAX_WEIGHT * product(far[site], op_pair[site][side])
        one_pair[site] = value.astype(jnp.bfloat16)
        value = near[(1,) + site].astype(jnp.float32) - RELAX_WEIGHT * products([(back_near[site], sent[(0,) + site])])
        one_near[site] = value.astype(jnp.bfloat16)

    for_sites(op_mine.shape[:3], first)


def product(field, weights):
    return jnp.dot(field, weights, preferred_element_type=jnp.float32)


def second_step(op_mine, rhs_mine, one_mine, one_pair, one_near, x_mine, site):
    sums = packed_stencil(op_mine, site, one_mine, [one_pair, one_near])
    return relaxed(x_mine[site], one_mine[site], rhs_mine[site], sums)


def third_kernel(op_mine, rhs_mine, field_mine, value_mine, field_pair, message, part_next):
    def third(site):
        sums = packed_stencil(op_mine, site, field_mine, [field_pair])
        part = relaxed(value_mine[site], field_mine[site], rhs_mine[site], sums)
        part_next[site] = part
        message[(0,) + site] = field_mine[site]
        message[(1,) + site] = part.astype(jnp.bfloat16)

    for_sites(op_mine.shape[:3], third)


def last_kernel(
    op_mine, op_pair, back_near, rhs_mine, sent, part_mine, part_pair, near, far, null,
    fine_out, coarse_out, one_mine, one_pair, one_near, x_mine, result, held, done,
):
    extent = op_mine.shape[:3]
    halfway(op_mine, op_pair, back_near, sent, part_mine, part_pair, near, far, one_mine, one_pair, one_near, x_mine)

    def second(site):
        value = second_step(op_mine, rhs_mine, one_mine, one_pair, one_near, x_mine, site)
        result[(0,) + site] = value.astype(jnp.bfloat16)

    for_sites(extent, second)
    times = held.shape[0]
    copy = pltpu.make_async_copy(result, coarse_out, done.at[times])
    copy.start()
    position = lax.axis_index("xy")
    column = [result[0, y, z, position] for y in range(extent[0]) for z in range(extent[1])]
    prolong(column, null, fine_out, held, done)
    copy.wait()


def last(shape, *operands):
    full, times = operands[5].shape, shape[0]
    return pl.pallas_call(
        last_kernel,
        in_specs=[pl.BlockSpec(memory_space=pltpu.VMEM)] * len(operands),
        out_specs=[pl.BlockSpec(memory_space=pl.ANY)] * 2,
        out_shape=[
            jax.ShapeDtypeStruct(shape, jnp.bfloat16),
            jax.ShapeDtypeStruct((1,) + full, jnp.bfloat16),
        ],
        scratch_shapes=[pltpu.VMEM(full, jnp.bfloat16)] * 3
        + [
            pltpu.VMEM(full, jnp.float32),
            pltpu.VMEM((1,) + full, jnp.bfloat16),
            pltpu.VMEM(shape, jnp.bfloat16),
            pltpu.SemaphoreType.DMA((times + 1,)),
        ],
        compiler_params=pltpu.CompilerParams(vmem_limit_bytes=KERNEL_VMEM),
        name="last",
    )(*[in_vmem(operand) for operand in operands])


def packed_depth(operator):
    blocks = 3 + sum(1 if length == 2 else 2 for length in operator.shape[2:5])
    return blocks * operator.shape[6]


def in_hbm(array):
    return pltpu.with_memory_space_constraint(array, pltpu.HBM)


def in_vmem(array):
    return pltpu.with_memory_space_constraint(array, pltpu.VMEM)


def kernel_call(kernel, name, outs, scratch, *operands, flops=0):
    return pl.pallas_call(
        kernel,
        in_specs=[pl.BlockSpec(memory_space=pltpu.VMEM)] * len(operands),
        out_specs=[pl.BlockSpec(memory_space=pltpu.VMEM)] * len(outs),
        out_shape=[pltpu.VMEM(shape, dtype) for shape, dtype in outs],
        scratch_shapes=[pltpu.VMEM(shape, dtype) for shape, dtype in scratch],
        compiler_params=pltpu.CompilerParams(vmem_limit_bytes=KERNEL_VMEM),
        cost_estimate=pl.CostEstimate(flops=flops, bytes_accessed=0, transcendentals=0) if flops else None,
        name=name,
    )(*[in_vmem(operand) for operand in operands])


def exchange_plan():
    slices, columns = lax.axis_size("zt"), lax.axis_size("xy")
    other = [i ^ 1 for i in range(slices)]
    across = [(i + 1 if i % 2 else i - 1) % slices for i in range(slices)]

    def permutation(target, turn=0):
        return [
            (i * columns + j, target[i] * columns + (j + turn) % columns) for i in range(slices) for j in range(columns)
        ]

    def send(array, target, turn=0):
        return lax.ppermute(array, ("zt", "xy"), permutation(target, turn))

    far = [other[across[i]] for i in range(slices)]
    return send, list(range(slices)), other, across, far


def per_device(fine_vectors, null_vectors, coarse_operator):
    send, same, other, across, far = exchange_plan()
    columns = lax.axis_size("xy")
    extent = coarse_operator.shape[2:5]
    bf16, f32 = jnp.bfloat16, jnp.float32
    own, null_kept, operator, block = restrict(fine_vectors, null_vectors, coarse_operator)
    full = extent + own.shape[1:]
    if columns == 2:
        parts = [own, send(own, same, 1), send(own, other), send(own, other, 1)]
    else:
        every = lax.all_gather(own, "xy")
        parts = [every, send(every, other)]
    back_near = send(block, across)
    op_pair = send(operator, other)
    rhs_mine, rhs_pair, start_mine, start_pair, sent, part_mine = kernel_call(
        functools.partial(gather_kernel, len(parts) // 2),
        "gather",
        [(full, bf16)] * 4 + [((2,) + full, bf16), (full, f32)],
        [],
        operator,
        *parts,
        flops=GATHER_FLOPS,
    )
    near_message, far_field = send(sent, across), send(start_mine, far)
    (part_pair, packed_mine, packed_pair) = kernel_call(
        first_pair_kernel,
        "pair_one",
        [(full, f32)] + [(extent + (packed_depth(operator), operator.shape[6]), bf16)] * 2,
        [],
        operator, op_pair, rhs_pair, start_pair, start_mine,
    )
    field_mine, value_mine = kernel_call(
        second_kernel,
        "second",
        [(full, bf16), (full, f32)],
        [(full, bf16)] * 3 + [(full, f32)],
        packed_mine, packed_pair, back_near, rhs_mine, sent, part_mine, part_pair, near_message, far_field,
    )
    field_pair = send(field_mine, other)
    sent, part_mine = kernel_call(
        third_kernel, "third", [((2,) + full, bf16), (full, f32)], [],
        packed_mine, rhs_mine, field_mine, value_mine, field_pair,
    )
    near_message, far_field = send(sent, across), send(field_mine, far)
    (part_pair,) = kernel_call(
        second_pair_kernel, "pair_two", [(full, f32)], [],
        packed_pair, rhs_pair, field_pair, field_mine,
    )
    fine_correction, coarse_iterate = last(
        fine_vectors.shape,
        packed_mine, packed_pair, back_near, rhs_mine, sent, part_mine, part_pair, near_message, far_field, null_kept,
    )
    return (fine_correction, coarse_iterate)


def solution(mesh):
    return jax.shard_map(
        per_device,
        mesh=mesh,
        in_specs=(
            P("zt", None, None, None, "xy"),
            P("zt", None, None, None, "xy"),
            P("zt", None, None, None, None, None, None),
        ),
        out_specs=(P("zt", None, None, None, "xy"), P("zt", None, None, None, None, None)),
        check_vma=False,
    )
```

```python
import functools

import jax
import jax.numpy as jnp
from jax import lax
from jax.experimental import pallas as pl
from jax.experimental.pallas import tpu as pltpu
from jax.sharding import PartitionSpec as P

CZ = 2
APPLIES = 4
RELAX_WEIGHT = 0.3
DIAGONAL_SHIFT = 3.0
LANES = (((1,), (1,)), ((), ()))
KERNEL_VMEM = 16 * 1024 * 1024
GATHER_FLOPS = 10**10


def aggregate_ids(shape, coarse_y):
    site = lax.broadcasted_iota(jnp.int32, shape, len(shape) - 1)
    row = 4 * coarse_y
    y = lax.rem(site, row) // 4
    z = lax.rem(site, row * 4 * CZ) // (row * 4)
    return y * CZ + z


def restrict_kernel(coarse_y, fine_hbm, null_hbm, operator_hbm, out_ref, null_ref, operator, fine_ref, loaded):
    aggregates = coarse_y * CZ
    times, _, _, rhs, sites = fine_ref.shape
    vectors = null_ref.shape[3]
    loads = []
    for t in range(times):
        loads.append(pltpu.make_async_copy(fine_hbm.at[t], fine_ref.at[t], loaded.at[2 * t]))
        loads.append(pltpu.make_async_copy(null_hbm.at[t], null_ref.at[t], loaded.at[2 * t + 1]))
    loads.append(pltpu.make_async_copy(operator_hbm, operator, loaded.at[2 * times]))
    for load in loads:
        load.start()
    ids = aggregate_ids((2 * rhs, sites), coarse_y)
    masks = [(ids == a).astype(jnp.float32).astype(jnp.bfloat16) for a in range(aggregates)]
    sums = [None, None]
    for t in range(times):
        loads[2 * t].wait()
        loads[2 * t + 1].wait()
        for h in range(2):
            left, right = [], []
            for c in range(h * 6, h * 6 + 6):
                fine = jnp.concatenate([fine_ref[t, 0, c], fine_ref[t, 1, c]], axis=0)
                left.append(jnp.concatenate([fine * m for m in masks], axis=0))
                right.append(jnp.concatenate([null_ref[t, 0, c], null_ref[t, 1, c]], axis=0))
            part = lax.dot_general(
                jnp.concatenate(left, axis=1),
                jnp.concatenate(right, axis=1),
                LANES,
                preferred_element_type=jnp.float32,
            )
            sums[h] = part if sums[h] is None else sums[h] + part
    for a in range(aggregates):
        real, imag = [], []
        for h in range(2):
            top = sums[h][a * 2 * rhs : a * 2 * rhs + rhs]
            low = sums[h][a * 2 * rhs + rhs : (a + 1) * 2 * rhs]
            real.append(top[:, :vectors] + low[:, vectors:])
            imag.append(low[:, :vectors] - top[:, vectors:])
        out_ref[a] = jnp.concatenate(real + imag, axis=1).astype(out_ref.dtype)
    loads[-1].wait()


def restrict(fine, null, operator):
    times, _, _, rhs, sites = fine.shape
    coarse_y = sites // (64 * CZ)
    return pl.pallas_call(
        functools.partial(restrict_kernel, coarse_y),
        in_specs=[pl.BlockSpec(memory_space=pl.ANY)] * 3,
        out_specs=[pl.BlockSpec(memory_space=pltpu.VMEM)] * 3,
        out_shape=[
            pltpu.VMEM((coarse_y * CZ, rhs, 4 * null.shape[3]), jnp.bfloat16),
            pltpu.VMEM(null.shape, null.dtype),
            pltpu.VMEM(operator.shape, operator.dtype),
        ],
        scratch_shapes=[pltpu.VMEM(fine.shape, fine.dtype), pltpu.SemaphoreType.DMA((2 * times + 1,))],
        compiler_params=pltpu.CompilerParams(vmem_limit_bytes=KERNEL_VMEM),
        name="restrict",
    )(in_hbm(fine), in_hbm(null), in_hbm(operator))


def prolong(column, null_ref, out_ref, held, done):
    coarse_y = len(column) // CZ
    times, _, _, rhs, sites = held.shape
    vectors = null_ref.shape[3]
    ids = aggregate_ids((2 * vectors, sites), coarse_y)
    masks = [(lax.rem(ids, CZ) == z).astype(jnp.float32).astype(jnp.bfloat16) for z in range(CZ)]
    rows = aggregate_ids((2 * rhs, sites), coarse_y) // CZ
    mixers = []
    for h in range(2):
        mixer = []
        for y in range(coarse_y):
            real = [column[y * CZ + z][:, h * vectors : (h + 1) * vectors] for z in range(CZ)]
            imag = [column[y * CZ + z][:, (2 + h) * vectors : (3 + h) * vectors] for z in range(CZ)]
            mixer.append(jnp.concatenate([part for z in range(CZ) for part in (real[z], -imag[z])], axis=1))
            mixer.append(jnp.concatenate([part for z in range(CZ) for part in (imag[z], real[z])], axis=1))
        mixers.append(jnp.concatenate(mixer, axis=0))
    copies = []
    for t in range(times):
        for c in range(12):
            null = jnp.concatenate([null_ref[t, 0, c], null_ref[t, 1, c]], axis=0)
            null = jnp.concatenate([null * mask for mask in masks], axis=0)
            every = jnp.dot(mixers[c // 6], null, preferred_element_type=jnp.float32)
            result = every[: 2 * rhs]
            for y in range(1, coarse_y):
                result = jnp.where(rows == y, every[y * 2 * rhs : (y + 1) * 2 * rhs], result)
            result = result.astype(held.dtype)
            held[t, 0, c] = result[:rhs]
            held[t, 1, c] = result[rhs:]
        copies.append(pltpu.make_async_copy(held.at[t], out_ref.at[t], done.at[t]))
        copies[-1].start()
    for copy in copies:
        copy.wait()


def time_sides(even_slice):
    parity = lax.rem(lax.axis_index("zt"), 2)
    if not even_slice:
        parity = 1 - parity
    return 1 + parity, 2 - parity


def for_sites(extent, body):
    for y in range(extent[0]):
        for z in range(extent[1]):
            if extent[2] <= 2:
                for x in range(extent[2]):
                    body((y, z, x))
            else:
                lax.fori_loop(0, extent[2], lambda x, c, y=y, z=z: (body((y, z, x)), c)[1], 0)


def nearby(site, extent):
    found = [site]
    for axis in range(3):
        for step in [1] if extent[axis] == 2 else [1, extent[axis] - 1]:
            moved = site[axis] + step
            moved = lax.rem(moved, extent[axis]) if axis == 2 else moved % extent[axis]
            found.append(site[:axis] + (moved,) + site[axis + 1 :])
    return found


def around(operator, site, extent):
    blocks = [operator[(0, 0) + site]]
    for axis in range(3):
        ahead, behind = operator[(0, 3 + 2 * axis) + site], operator[(0, 4 + 2 * axis) + site]
        if extent[axis] == 2:
            both = ahead.astype(jnp.float32) + behind.astype(jnp.float32)
            blocks.append(both.astype(jnp.bfloat16))
        else:
            blocks += [ahead, behind]
    return list(zip(blocks, nearby(site, extent)))


def products(pairs):
    return lax.dot_general(
        jnp.concatenate([field for _, field in pairs], axis=1),
        jnp.concatenate([block for block, _ in pairs], axis=1),
        LANES,
        preferred_element_type=jnp.float32,
    )


def packed(operator, site, times):
    blocks = [block for block, _ in around(operator, site, operator.shape[2:5])]
    blocks += [operator[(0, d) + site] for d in times]
    return jnp.concatenate([block.T for block in blocks], axis=0)


def packed_stencil(weights, site, here, times):
    extent = weights.shape[:3]
    fields = [here[near] for near in nearby(site, extent)] + [field[site] for field in times]
    depth = len(fields) * weights.shape[4]
    return jnp.dot(jnp.concatenate(fields, axis=1), weights[site][:depth], preferred_element_type=jnp.float32)


def stencil(operator, site, here, times):
    extent = operator.shape[2:5]
    pairs = [(block, here[near]) for block, near in around(operator, site, extent)]
    pairs += [(operator[(0, d) + site], field[site]) for d, field in times]
    return products(pairs)


def relaxed(value, rounded, target, sums):
    image = sums + DIAGONAL_SHIFT * rounded.astype(jnp.float32)
    return value + RELAX_WEIGHT * (target.astype(jnp.float32) - image)


def block_kernel(op_mine, op_pair, block):
    _, odd = time_sides(True)
    _, pair_odd = time_sides(False)
    first = lax.axis_index("zt") < 2

    @pl.when(first)
    def _():
        block[...] = op_pair[0, pair_odd]

    @pl.when(jnp.logical_not(first))
    def _():
        block[...] = op_mine[0, odd]


def gather_kernel(pieces, operator, *refs):
    parts, (rhs_mine, rhs_pair, start_mine, start_pair, message, part_mine) = refs[: 2 * pieces], refs[2 * pieces :]
    extent = operator.shape[2:5]
    position = lax.axis_index("xy")
    even, _ = time_sides(True)
    parts = parts[::-1]
    for whole, held in ((rhs_mine, parts[:pieces]), (rhs_pair, parts[pieces:])):
        for y in range(extent[0]):
            for z in range(extent[1]):
                for x in range(extent[2]):
                    if pieces == 1:
                        whole[y, z, x] = held[0][x, y * extent[1] + z]
                    else:
                        whole[y, z, lax.rem(position + x, pieces)] = held[x][y * extent[1] + z]

    def begin(site):
        start_mine[site] = (RELAX_WEIGHT * rhs_mine[site].astype(jnp.float32)).astype(jnp.bfloat16)
        message[(0,) + site] = start_mine[site]
        start_pair[site] = (RELAX_WEIGHT * rhs_pair[site].astype(jnp.float32)).astype(jnp.bfloat16)

    for_sites(extent, begin)
    here = start_mine

    def step(site):
        sums = stencil(operator, site, here, [(even, start_pair)])
        value = RELAX_WEIGHT * rhs_mine[site].astype(jnp.float32)
        part = relaxed(value, here[site], rhs_mine[site], sums)
        part_mine[site] = part
        message[(1,) + site] = part.astype(jnp.bfloat16)

    for_sites(extent, step)


def first_pair_kernel(op_mine, op_pair, rhs_pair, here, other, part_pair, packed_mine, packed_pair):
    sides, pair_sides = time_sides(True), time_sides(False)

    def step(site):
        packed_mine[site] = packed(op_mine, site, sides)
        packed_pair[site] = packed(op_pair, site, pair_sides)
        sums = packed_stencil(packed_pair, site, here, [other])
        value = RELAX_WEIGHT * rhs_pair[site].astype(jnp.float32)
        part_pair[site] = relaxed(value, here[site], rhs_pair[site], sums)

    for_sites(op_mine.shape[2:5], step)


def second_pair_kernel(packed_pair, rhs_pair, here, other, part_pair):
    def step(site):
        sums = packed_stencil(packed_pair, site, here, [other])
        part_pair[site] = relaxed(here[site].astype(jnp.float32), here[site], rhs_pair[site], sums)

    for_sites(packed_pair.shape[:3], step)


def second_kernel(
    op_mine, op_pair, back_near, rhs_mine, sent, part_mine, part_pair, near, far,
    field_mine, value_mine, one_mine, one_pair, one_near, x_mine,
):
    halfway(op_mine, op_pair, back_near, sent, part_mine, part_pair, near, far, one_mine, one_pair, one_near, x_mine)

    def second(site):
        value = second_step(op_mine, rhs_mine, one_mine, one_pair, one_near, x_mine, site)
        value_mine[site] = value
        field_mine[site] = value.astype(jnp.bfloat16)

    for_sites(op_mine.shape[:3], second)


def halfway(op_mine, op_pair, back_near, sent, part_mine, part_pair, near, far, one_mine, one_pair, one_near, x_mine):
    depth, columns = op_mine.shape[3:]
    side = slice(depth - columns, depth)

    def first(site):
        value = part_mine[site] - RELAX_WEIGHT * product(near[(0,) + site], op_mine[site][side])
        x_mine[site] = value
        one_mine[site] = value.astype(jnp.bfloat16)
        value = part_pair[site] - RELAX_WEIGHT * product(far[site], op_pair[site][side])
        one_pair[site] = value.astype(jnp.bfloat16)
        value = near[(1,) + site].astype(jnp.float32) - RELAX_WEIGHT * products([(back_near[site], sent[(0,) + site])])
        one_near[site] = value.astype(jnp.bfloat16)

    for_sites(op_mine.shape[:3], first)


def product(field, weights):
    return jnp.dot(field, weights, preferred_element_type=jnp.float32)


def second_step(op_mine, rhs_mine, one_mine, one_pair, one_near, x_mine, site):
    sums = packed_stencil(op_mine, site, one_mine, [one_pair, one_near])
    return relaxed(x_mine[site], one_mine[site], rhs_mine[site], sums)


def third_kernel(op_mine, rhs_mine, field_mine, value_mine, field_pair, message, part_next):
    def third(site):
        sums = packed_stencil(op_mine, site, field_mine, [field_pair])
        part = relaxed(value_mine[site], field_mine[site], rhs_mine[site], sums)
        part_next[site] = part
        message[(0,) + site] = field_mine[site]
        message[(1,) + site] = part.astype(jnp.bfloat16)

    for_sites(op_mine.shape[:3], third)


def last_kernel(
    op_mine, op_pair, back_near, rhs_mine, sent, part_mine, part_pair, near, far, null,
    fine_out, coarse_out, one_mine, one_pair, one_near, x_mine, result, held, done,
):
    extent = op_mine.shape[:3]
    halfway(op_mine, op_pair, back_near, sent, part_mine, part_pair, near, far, one_mine, one_pair, one_near, x_mine)

    def second(site):
        value = second_step(op_mine, rhs_mine, one_mine, one_pair, one_near, x_mine, site)
        result[(0,) + site] = value.astype(jnp.bfloat16)

    for_sites(extent, second)
    times = held.shape[0]
    copy = pltpu.make_async_copy(result, coarse_out, done.at[times])
    copy.start()
    position = lax.axis_index("xy")
    column = [result[0, y, z, position] for y in range(extent[0]) for z in range(extent[1])]
    prolong(column, null, fine_out, held, done)
    copy.wait()


def last(shape, *operands):
    full, times = operands[5].shape, shape[0]
    return pl.pallas_call(
        last_kernel,
        in_specs=[pl.BlockSpec(memory_space=pltpu.VMEM)] * len(operands),
        out_specs=[pl.BlockSpec(memory_space=pl.ANY)] * 2,
        out_shape=[
            jax.ShapeDtypeStruct(shape, jnp.bfloat16),
            jax.ShapeDtypeStruct((1,) + full, jnp.bfloat16),
        ],
        scratch_shapes=[pltpu.VMEM(full, jnp.bfloat16)] * 3
        + [
            pltpu.VMEM(full, jnp.float32),
            pltpu.VMEM((1,) + full, jnp.bfloat16),
            pltpu.VMEM(shape, jnp.bfloat16),
            pltpu.SemaphoreType.DMA((times + 1,)),
        ],
        compiler_params=pltpu.CompilerParams(vmem_limit_bytes=KERNEL_VMEM),
        name="last",
    )(*[in_vmem(operand) for operand in operands])


def packed_depth(operator):
    blocks = 3 + sum(1 if length == 2 else 2 for length in operator.shape[2:5])
    return blocks * operator.shape[6]


def in_hbm(array):
    return pltpu.with_memory_space_constraint(array, pltpu.HBM)


def in_vmem(array):
    return pltpu.with_memory_space_constraint(array, pltpu.VMEM)


def kernel_call(kernel, name, outs, scratch, *operands, flops=0):
    return pl.pallas_call(
        kernel,
        in_specs=[pl.BlockSpec(memory_space=pltpu.VMEM)] * len(operands),
        out_specs=[pl.BlockSpec(memory_space=pltpu.VMEM)] * len(outs),
        out_shape=[pltpu.VMEM(shape, dtype) for shape, dtype in outs],
        scratch_shapes=[pltpu.VMEM(shape, dtype) for shape, dtype in scratch],
        compiler_params=pltpu.CompilerParams(vmem_limit_bytes=KERNEL_VMEM),
        cost_estimate=pl.CostEstimate(flops=flops, bytes_accessed=0, transcendentals=0) if flops else None,
        name=name,
    )(*[in_vmem(operand) for operand in operands])


def exchange_plan():
    slices, columns = lax.axis_size("zt"), lax.axis_size("xy")
    other = [i ^ 1 for i in range(slices)]
    across = [(i + 1 if i % 2 else i - 1) % slices for i in range(slices)]

    def permutation(target, turn=0):
        return [
            (i * columns + j, target[i] * columns + (j + turn) % columns) for i in range(slices) for j in range(columns)
        ]

    def send(array, target, turn=0):
        return lax.ppermute(array, ("zt", "xy"), permutation(target, turn))

    far = [other[across[i]] for i in range(slices)]
    return send, list(range(slices)), other, across, far


def per_device(fine_vectors, null_vectors, coarse_operator):
    send, same, other, across, far = exchange_plan()
    columns = lax.axis_size("xy")
    extent = coarse_operator.shape[2:5]
    bf16, f32 = jnp.bfloat16, jnp.float32
    own, null_kept, operator = restrict(fine_vectors, null_vectors, coarse_operator)
    full = extent + own.shape[1:]
    if columns == 2:
        corner, pair, beside = send(own, other, 1), send(own, other), send(own, same, 1)
        parts = [own, beside, pair, corner]
    else:
        every = lax.all_gather(own, "xy")
        parts = [every, send(every, other)]
    op_pair = send(coarse_operator, other)
    (block,) = kernel_call(block_kernel, "block", [(operator.shape[2:], bf16)], [], operator, op_pair)
    back_near = send(block, [across[1], across[0]] + across[2:])
    rhs_mine, rhs_pair, start_mine, start_pair, sent, part_mine = kernel_call(
        functools.partial(gather_kernel, len(parts) // 2),
        "gather",
        [(full, bf16)] * 4 + [((2,) + full, bf16), (full, f32)],
        [],
        operator,
        *parts[::-1],
        flops=GATHER_FLOPS,
    )
    near_message, far_field = send(sent, across), send(start_mine, far)
    (part_pair, packed_mine, packed_pair) = kernel_call(
        first_pair_kernel,
        "pair_one",
        [(full, f32)] + [(extent + (packed_depth(operator), operator.shape[6]), bf16)] * 2,
        [],
        operator, op_pair, rhs_pair, start_pair, start_mine,
    )
    field_mine, value_mine = kernel_call(
        second_kernel,
        "second",
        [(full, bf16), (full, f32)],
        [(full, bf16)] * 3 + [(full, f32)],
        packed_mine, packed_pair, back_near, rhs_mine, sent, part_mine, part_pair, near_message, far_field,
    )
    field_pair = send(field_mine, other)
    sent, part_mine = kernel_call(
        third_kernel, "third", [((2,) + full, bf16), (full, f32)], [],
        packed_mine, rhs_mine, field_mine, value_mine, field_pair,
    )
    near_message, far_field = send(sent, across), send(field_mine, far)
    (part_pair,) = kernel_call(
        second_pair_kernel, "pair_two", [(full, f32)], [],
        packed_pair, rhs_pair, field_pair, field_mine,
    )
    fine_correction, coarse_iterate = last(
        fine_vectors.shape,
        packed_mine, packed_pair, back_near, rhs_mine, sent, part_mine, part_pair, near_message, far_field, null_kept,
    )
    return (fine_correction, coarse_iterate)


def solution(mesh):
    return jax.shard_map(
        per_device,
        mesh=mesh,
        in_specs=(
            P("zt", None, None, None, "xy"),
            P("zt", None, None, None, "xy"),
            P("zt", None, None, None, None, None, None),
        ),
        out_specs=(P("zt", None, None, None, "xy"), P("zt", None, None, None, None, None)),
        check_vma=False,
    )
```

```python
import functools

import jax
import jax.numpy as jnp
from jax import lax
from jax.experimental import pallas as pl
from jax.experimental.pallas import tpu as pltpu
from jax.sharding import PartitionSpec as P

CZ = 2
APPLIES = 4
RELAX_WEIGHT = 0.3
DIAGONAL_SHIFT = 3.0
LANES = (((1,), (1,)), ((), ()))
KERNEL_VMEM = 16 * 1024 * 1024
GATHER_FLOPS = 10**10


def aggregate_ids(shape, coarse_y):
    site = lax.broadcasted_iota(jnp.int32, shape, len(shape) - 1)
    row = 4 * coarse_y
    y = lax.rem(site, row) // 4
    z = lax.rem(site, row * 4 * CZ) // (row * 4)
    return y * CZ + z


def restrict_kernel(coarse_y, fine_hbm, null_hbm, operator_hbm, out_ref, null_ref, operator, fine_ref, loaded):
    aggregates = coarse_y * CZ
    times, _, _, rhs, sites = fine_ref.shape
    vectors = null_ref.shape[3]
    loads = []
    for t in range(times):
        loads.append(pltpu.make_async_copy(fine_hbm.at[t], fine_ref.at[t], loaded.at[2 * t]))
        loads.append(pltpu.make_async_copy(null_hbm.at[t], null_ref.at[t], loaded.at[2 * t + 1]))
    loads.append(pltpu.make_async_copy(operator_hbm, operator, loaded.at[2 * times]))
    for load in loads:
        load.start()
    ids = aggregate_ids((2 * rhs, sites), coarse_y)
    masks = [(ids == a).astype(jnp.float32).astype(jnp.bfloat16) for a in range(aggregates)]
    sums = [None, None]
    for t in range(times):
        loads[2 * t].wait()
        loads[2 * t + 1].wait()
        for h in range(2):
            left, right = [], []
            for c in range(h * 6, h * 6 + 6):
                fine = jnp.concatenate([fine_ref[t, 0, c], fine_ref[t, 1, c]], axis=0)
                left.append(jnp.concatenate([fine * m for m in masks], axis=0))
                right.append(jnp.concatenate([null_ref[t, 0, c], null_ref[t, 1, c]], axis=0))
            part = lax.dot_general(
                jnp.concatenate(left, axis=1),
                jnp.concatenate(right, axis=1),
                LANES,
                preferred_element_type=jnp.float32,
            )
            sums[h] = part if sums[h] is None else sums[h] + part
    for a in range(aggregates):
        real, imag = [], []
        for h in range(2):
            top = sums[h][a * 2 * rhs : a * 2 * rhs + rhs]
            low = sums[h][a * 2 * rhs + rhs : (a + 1) * 2 * rhs]
            real.append(top[:, :vectors] + low[:, vectors:])
            imag.append(low[:, :vectors] - top[:, vectors:])
        out_ref[a] = jnp.concatenate(real + imag, axis=1).astype(out_ref.dtype)
    loads[-1].wait()


def restrict(fine, null, operator):
    times, _, _, rhs, sites = fine.shape
    coarse_y = sites // (64 * CZ)
    return pl.pallas_call(
        functools.partial(restrict_kernel, coarse_y),
        in_specs=[pl.BlockSpec(memory_space=pl.ANY)] * 3,
        out_specs=[pl.BlockSpec(memory_space=pltpu.VMEM)] * 3,
        out_shape=[
            pltpu.VMEM((coarse_y * CZ, rhs, 4 * null.shape[3]), jnp.bfloat16),
            pltpu.VMEM(null.shape, null.dtype),
            pltpu.VMEM(operator.shape, operator.dtype),
        ],
        scratch_shapes=[pltpu.VMEM(fine.shape, fine.dtype), pltpu.SemaphoreType.DMA((2 * times + 1,))],
        compiler_params=pltpu.CompilerParams(vmem_limit_bytes=KERNEL_VMEM),
        name="restrict",
    )(in_hbm(fine), in_hbm(null), in_hbm(operator))


def prolong(column, null_ref, out_ref, held, done):
    coarse_y = len(column) // CZ
    times, _, _, rhs, sites = held.shape
    vectors = null_ref.shape[3]
    ids = aggregate_ids((2 * vectors, sites), coarse_y)
    masks = [(lax.rem(ids, CZ) == z).astype(jnp.float32).astype(jnp.bfloat16) for z in range(CZ)]
    rows = aggregate_ids((2 * rhs, sites), coarse_y) // CZ
    mixers = []
    for h in range(2):
        mixer = []
        for y in range(coarse_y):
            real = [column[y * CZ + z][:, h * vectors : (h + 1) * vectors] for z in range(CZ)]
            imag = [column[y * CZ + z][:, (2 + h) * vectors : (3 + h) * vectors] for z in range(CZ)]
            mixer.append(jnp.concatenate([part for z in range(CZ) for part in (real[z], -imag[z])], axis=1))
            mixer.append(jnp.concatenate([part for z in range(CZ) for part in (imag[z], real[z])], axis=1))
        mixers.append(jnp.concatenate(mixer, axis=0))
    copies = []
    for t in range(times):
        for c in range(12):
            null = jnp.concatenate([null_ref[t, 0, c], null_ref[t, 1, c]], axis=0)
            null = jnp.concatenate([null * mask for mask in masks], axis=0)
            every = jnp.dot(mixers[c // 6], null, preferred_element_type=jnp.float32)
            result = every[: 2 * rhs]
            for y in range(1, coarse_y):
                result = jnp.where(rows == y, every[y * 2 * rhs : (y + 1) * 2 * rhs], result)
            result = result.astype(held.dtype)
            held[t, 0, c] = result[:rhs]
            held[t, 1, c] = result[rhs:]
        copies.append(pltpu.make_async_copy(held.at[t], out_ref.at[t], done.at[t]))
        copies[-1].start()
    for copy in copies:
        copy.wait()


def time_sides(even_slice):
    parity = lax.rem(lax.axis_index("zt"), 2)
    if not even_slice:
        parity = 1 - parity
    return 1 + parity, 2 - parity


def for_sites(extent, body):
    for y in range(extent[0]):
        for z in range(extent[1]):
            if extent[2] <= 2:
                for x in range(extent[2]):
                    body((y, z, x))
            else:
                lax.fori_loop(0, extent[2], lambda x, c, y=y, z=z: (body((y, z, x)), c)[1], 0)


def nearby(site, extent):
    found = [site]
    for axis in range(3):
        for step in [1] if extent[axis] == 2 else [1, extent[axis] - 1]:
            moved = site[axis] + step
            moved = lax.rem(moved, extent[axis]) if axis == 2 else moved % extent[axis]
            found.append(site[:axis] + (moved,) + site[axis + 1 :])
    return found


def around(operator, site, extent):
    blocks = [operator[(0, 0) + site]]
    for axis in range(3):
        ahead, behind = operator[(0, 3 + 2 * axis) + site], operator[(0, 4 + 2 * axis) + site]
        if extent[axis] == 2:
            both = ahead.astype(jnp.float32) + behind.astype(jnp.float32)
            blocks.append(both.astype(jnp.bfloat16))
        else:
            blocks += [ahead, behind]
    return list(zip(blocks, nearby(site, extent)))


def products(pairs):
    return lax.dot_general(
        jnp.concatenate([field for _, field in pairs], axis=1),
        jnp.concatenate([block for block, _ in pairs], axis=1),
        LANES,
        preferred_element_type=jnp.float32,
    )


def packed(operator, site, times):
    blocks = [block for block, _ in around(operator, site, operator.shape[2:5])]
    blocks += [operator[(0, d) + site] for d in times]
    return jnp.concatenate([block.T for block in blocks], axis=0)


def packed_stencil(weights, site, here, times):
    extent = weights.shape[:3]
    fields = [here[near] for near in nearby(site, extent)] + [field[site] for field in times]
    depth = len(fields) * weights.shape[4]
    return jnp.dot(jnp.concatenate(fields, axis=1), weights[site][:depth], preferred_element_type=jnp.float32)


def stencil(operator, site, here, times):
    extent = operator.shape[2:5]
    pairs = [(block, here[near]) for block, near in around(operator, site, extent)]
    pairs += [(operator[(0, d) + site], field[site]) for d, field in times]
    return products(pairs)


def relaxed(value, rounded, target, sums):
    image = sums + DIAGONAL_SHIFT * rounded.astype(jnp.float32)
    return value + RELAX_WEIGHT * (target.astype(jnp.float32) - image)


def block_kernel(op_mine, op_pair, block):
    _, odd = time_sides(True)
    _, pair_odd = time_sides(False)
    first = lax.axis_index("zt") < 2

    @pl.when(first)
    def _():
        block[...] = op_pair[0, pair_odd]

    @pl.when(jnp.logical_not(first))
    def _():
        block[...] = op_mine[0, odd]


def gather_kernel(pieces, operator, *refs):
    parts, (rhs_mine, rhs_pair, start_mine, start_pair, message, part_mine) = refs[: 2 * pieces], refs[2 * pieces :]
    extent = operator.shape[2:5]
    position = lax.axis_index("xy")
    even, _ = time_sides(True)
    parts = parts[::-1]
    for whole, held in ((rhs_mine, parts[:pieces]), (rhs_pair, parts[pieces:])):
        for y in range(extent[0]):
            for z in range(extent[1]):
                for x in range(extent[2]):
                    if pieces == 1:
                        whole[y, z, x] = held[0][x, y * extent[1] + z]
                    else:
                        whole[y, z, lax.rem(position + x, pieces)] = held[x][y * extent[1] + z]

    def begin(site):
        start_mine[site] = (RELAX_WEIGHT * rhs_mine[site].astype(jnp.float32)).astype(jnp.bfloat16)
        message[(0,) + site] = start_mine[site]
        start_pair[site] = (RELAX_WEIGHT * rhs_pair[site].astype(jnp.float32)).astype(jnp.bfloat16)

    for_sites(extent, begin)
    here = start_mine

    def step(site):
        sums = stencil(operator, site, here, [(even, start_pair)])
        value = RELAX_WEIGHT * rhs_mine[site].astype(jnp.float32)
        part = relaxed(value, here[site], rhs_mine[site], sums)
        part_mine[site] = part
        message[(1,) + site] = part.astype(jnp.bfloat16)

    for_sites(extent, step)


def first_pair_kernel(op_mine, op_pair, rhs_pair, here, other, part_pair, packed_mine, packed_pair):
    sides, pair_sides = time_sides(True), time_sides(False)

    def step(site):
        packed_mine[site] = packed(op_mine, site, sides)
        packed_pair[site] = packed(op_pair, site, pair_sides)
        sums = packed_stencil(packed_pair, site, here, [other])
        value = RELAX_WEIGHT * rhs_pair[site].astype(jnp.float32)
        part_pair[site] = relaxed(value, here[site], rhs_pair[site], sums)

    for_sites(op_mine.shape[2:5], step)


def second_pair_kernel(packed_pair, rhs_pair, here, other, part_pair):
    def step(site):
        sums = packed_stencil(packed_pair, site, here, [other])
        part_pair[site] = relaxed(here[site].astype(jnp.float32), here[site], rhs_pair[site], sums)

    for_sites(packed_pair.shape[:3], step)


def second_near_kernel(op_mine, back_near, rhs_mine, sent, part_mine, near, rest, one_mine, one_near):
    def first(site):
        value = near_step(op_mine, part_mine, near.at[0], site)
        rest[site] = value
        one_mine[site] = value.astype(jnp.bfloat16)
        one_near[site] = return_step(back_near, sent, near, site)

    for_sites(op_mine.shape[:3], first)

    def second(site):
        sums = packed_stencil(op_mine, site, one_mine, []) + side_product(one_near, op_mine, site, 1)
        rest[site] = relaxed(rest[site], one_mine[site], rhs_mine[site], sums)

    for_sites(op_mine.shape[:3], second)


def second_far_kernel(op_mine, op_pair, part_pair, far, rest, field_mine, value_mine):
    def step(site):
        one_pair = near_step(op_pair, part_pair, far, site).astype(jnp.bfloat16)
        sums = jnp.dot(one_pair, op_mine[site][side_rows(op_mine, 2)], preferred_element_type=jnp.float32)
        value = rest[site] - RELAX_WEIGHT * sums
        value_mine[site] = value
        field_mine[site] = value.astype(jnp.bfloat16)

    for_sites(op_mine.shape[:3], step)


def side_rows(weights, last):
    depth, columns = weights.shape[3:]
    return slice(depth - last * columns, depth - (last - 1) * columns)


def side_product(field, weights, site, last):
    return jnp.dot(field[site], weights[site][side_rows(weights, last)], preferred_element_type=jnp.float32)


def near_step(weights, part, received, site):
    return part[site] - RELAX_WEIGHT * side_product(received, weights, site, 1)


def return_step(back_near, sent, near, site):
    value = near[(1,) + site].astype(jnp.float32) - RELAX_WEIGHT * products([(back_near[site], sent[(0,) + site])])
    return value.astype(jnp.bfloat16)


def third_own_kernel(op_mine, rhs_mine, field_mine, value_mine, rest):
    def step(site):
        sums = packed_stencil(op_mine, site, field_mine, [])
        rest[site] = relaxed(value_mine[site], field_mine[site], rhs_mine[site], sums)

    for_sites(op_mine.shape[:3], step)


def third_kernel(op_mine, rest, field_mine, field_pair, message, part_next):
    def step(site):
        part = rest[site] - RELAX_WEIGHT * side_product(field_pair, op_mine, site, 2)
        part_next[site] = part
        message[(0,) + site] = field_mine[site]
        message[(1,) + site] = part.astype(jnp.bfloat16)

    for_sites(op_mine.shape[:3], step)


def last_kernel(
    op_mine, op_pair, back_near, rhs_mine, sent, part_mine, part_pair, near, far, null,
    fine_out, coarse_out, one_mine, one_pair, one_near, x_mine, result, held, done,
):
    extent = op_mine.shape[:3]

    def first(site):
        value = near_step(op_mine, part_mine, near.at[0], site)
        x_mine[site] = value
        one_mine[site] = value.astype(jnp.bfloat16)
        one_pair[site] = near_step(op_pair, part_pair, far, site).astype(jnp.bfloat16)
        one_near[site] = return_step(back_near, sent, near, site)

    for_sites(extent, first)

    def second(site):
        sums = packed_stencil(op_mine, site, one_mine, [one_pair, one_near])
        value = relaxed(x_mine[site], one_mine[site], rhs_mine[site], sums)
        result[(0,) + site] = value.astype(jnp.bfloat16)

    for_sites(extent, second)
    times = held.shape[0]
    copy = pltpu.make_async_copy(result, coarse_out, done.at[times])
    copy.start()
    position = lax.axis_index("xy")
    column = [result[0, y, z, position] for y in range(extent[0]) for z in range(extent[1])]
    prolong(column, null, fine_out, held, done)
    copy.wait()


def last(shape, *operands):
    full, times = operands[5].shape, shape[0]
    return pl.pallas_call(
        last_kernel,
        in_specs=[pl.BlockSpec(memory_space=pltpu.VMEM)] * len(operands),
        out_specs=[pl.BlockSpec(memory_space=pl.ANY)] * 2,
        out_shape=[
            jax.ShapeDtypeStruct(shape, jnp.bfloat16),
            jax.ShapeDtypeStruct((1,) + full, jnp.bfloat16),
        ],
        scratch_shapes=[pltpu.VMEM(full, jnp.bfloat16)] * 3
        + [
            pltpu.VMEM(full, jnp.float32),
            pltpu.VMEM((1,) + full, jnp.bfloat16),
            pltpu.VMEM(shape, jnp.bfloat16),
            pltpu.SemaphoreType.DMA((times + 1,)),
        ],
        compiler_params=pltpu.CompilerParams(vmem_limit_bytes=KERNEL_VMEM),
        name="last",
    )(*[in_vmem(operand) for operand in operands])


def packed_depth(operator):
    blocks = 3 + sum(1 if length == 2 else 2 for length in operator.shape[2:5])
    return blocks * operator.shape[6]


def in_hbm(array):
    return pltpu.with_memory_space_constraint(array, pltpu.HBM)


def in_vmem(array):
    return pltpu.with_memory_space_constraint(array, pltpu.VMEM)


def kernel_call(kernel, name, outs, scratch, *operands, flops=0):
    return pl.pallas_call(
        kernel,
        in_specs=[pl.BlockSpec(memory_space=pltpu.VMEM)] * len(operands),
        out_specs=[pl.BlockSpec(memory_space=pltpu.VMEM)] * len(outs),
        out_shape=[pltpu.VMEM(shape, dtype) for shape, dtype in outs],
        scratch_shapes=[pltpu.VMEM(shape, dtype) for shape, dtype in scratch],
        compiler_params=pltpu.CompilerParams(vmem_limit_bytes=KERNEL_VMEM),
        cost_estimate=pl.CostEstimate(flops=flops, bytes_accessed=0, transcendentals=0) if flops else None,
        name=name,
    )(*[in_vmem(operand) for operand in operands])


def exchange_plan():
    slices, columns = lax.axis_size("zt"), lax.axis_size("xy")
    other = [i ^ 1 for i in range(slices)]
    across = [(i + 1 if i % 2 else i - 1) % slices for i in range(slices)]

    def permutation(target, turn=0):
        return [
            (i * columns + j, target[i] * columns + (j + turn) % columns) for i in range(slices) for j in range(columns)
        ]

    def send(array, target, turn=0):
        return lax.ppermute(array, ("zt", "xy"), permutation(target, turn))

    far = [other[across[i]] for i in range(slices)]
    return send, list(range(slices)), other, across, far


def per_device(fine_vectors, null_vectors, coarse_operator):
    send, same, other, across, far = exchange_plan()
    columns = lax.axis_size("xy")
    extent = coarse_operator.shape[2:5]
    bf16, f32 = jnp.bfloat16, jnp.float32
    own, null_kept, operator = restrict(fine_vectors, null_vectors, coarse_operator)
    full = extent + own.shape[1:]
    if columns == 2:
        corner, pair, beside = send(own, other, 1), send(own, other), send(own, same, 1)
        parts = [own, beside, pair, corner]
    else:
        every = lax.all_gather(own, "xy")
        parts = [every, send(every, other)]
    op_pair = send(coarse_operator, other)
    (block,) = kernel_call(block_kernel, "block", [(operator.shape[2:], bf16)], [], operator, op_pair)
    back_near = send(block, [across[1], across[0]] + across[2:])
    rhs_mine, rhs_pair, start_mine, start_pair, sent, part_mine = kernel_call(
        functools.partial(gather_kernel, len(parts) // 2),
        "gather",
        [(full, bf16)] * 4 + [((2,) + full, bf16), (full, f32)],
        [],
        operator,
        *parts[::-1],
        flops=GATHER_FLOPS,
    )
    near_message, far_field = send(sent, across), send(start_mine, far)
    (part_pair, packed_mine, packed_pair) = kernel_call(
        first_pair_kernel,
        "pair_one",
        [(full, f32)] + [(extent + (packed_depth(operator), operator.shape[6]), bf16)] * 2,
        [],
        operator, op_pair, rhs_pair, start_pair, start_mine,
    )
    (rest,) = kernel_call(
        second_near_kernel, "second_near", [(full, f32)], [(full, bf16)] * 2,
        packed_mine, back_near, rhs_mine, sent, part_mine, near_message,
    )
    field_mine, value_mine = kernel_call(
        second_far_kernel, "second_far", [(full, bf16), (full, f32)], [],
        packed_mine, packed_pair, part_pair, far_field, rest,
    )
    field_pair = send(field_mine, other)
    (rest,) = kernel_call(
        third_own_kernel, "third_own", [(full, f32)], [], packed_mine, rhs_mine, field_mine, value_mine,
    )
    sent, part_mine = kernel_call(
        third_kernel, "third", [((2,) + full, bf16), (full, f32)], [], packed_mine, rest, field_mine, field_pair,
    )
    near_message, far_field = send(sent, across), send(field_mine, far)
    (part_pair,) = kernel_call(
        second_pair_kernel, "pair_two", [(full, f32)], [],
        packed_pair, rhs_pair, field_pair, field_mine,
    )
    fine_correction, coarse_iterate = last(
        fine_vectors.shape,
        packed_mine, packed_pair, back_near, rhs_mine, sent, part_mine, part_pair, near_message, far_field, null_kept,
    )
    return (fine_correction, coarse_iterate)


def solution(mesh):
    return jax.shard_map(
        per_device,
        mesh=mesh,
        in_specs=(
            P("zt", None, None, None, "xy"),
            P("zt", None, None, None, "xy"),
            P("zt", None, None, None, None, None, None),
        ),
        out_specs=(P("zt", None, None, None, "xy"), P("zt", None, None, None, None, None)),
        check_vma=False,
    )
```

```python
import functools

import jax
import jax.numpy as jnp
from jax import lax
from jax.experimental import pallas as pl
from jax.experimental.pallas import tpu as pltpu
from jax.sharding import PartitionSpec as P

CZ = 2
APPLIES = 4
RELAX_WEIGHT = 0.3
DIAGONAL_SHIFT = 3.0
LANES = (((1,), (1,)), ((), ()))
KERNEL_VMEM = 16 * 1024 * 1024
GATHER_FLOPS = 10**10


def aggregate_ids(shape, coarse_y):
    site = lax.broadcasted_iota(jnp.int32, shape, len(shape) - 1)
    row = 4 * coarse_y
    y = lax.rem(site, row) // 4
    z = lax.rem(site, row * 4 * CZ) // (row * 4)
    return y * CZ + z


def restrict_kernel(coarse_y, fine_hbm, null_hbm, operator_hbm, out_ref, null_ref, operator, fine_ref, loaded):
    aggregates = coarse_y * CZ
    times, _, _, rhs, sites = fine_ref.shape
    vectors = null_ref.shape[3]
    loads = []
    for t in range(times):
        loads.append(pltpu.make_async_copy(fine_hbm.at[t], fine_ref.at[t], loaded.at[2 * t]))
        loads.append(pltpu.make_async_copy(null_hbm.at[t], null_ref.at[t], loaded.at[2 * t + 1]))
    loads.append(pltpu.make_async_copy(operator_hbm, operator, loaded.at[2 * times]))
    for load in loads:
        load.start()
    ids = aggregate_ids((2 * rhs, sites), coarse_y)
    masks = [(ids == a).astype(jnp.float32).astype(jnp.bfloat16) for a in range(aggregates)]
    sums = [None, None]
    for t in range(times):
        loads[2 * t].wait()
        loads[2 * t + 1].wait()
        for h in range(2):
            left, right = [], []
            for c in range(h * 6, h * 6 + 6):
                fine = jnp.concatenate([fine_ref[t, 0, c], fine_ref[t, 1, c]], axis=0)
                left.append(jnp.concatenate([fine * m for m in masks], axis=0))
                right.append(jnp.concatenate([null_ref[t, 0, c], null_ref[t, 1, c]], axis=0))
            part = lax.dot_general(
                jnp.concatenate(left, axis=1),
                jnp.concatenate(right, axis=1),
                LANES,
                preferred_element_type=jnp.float32,
            )
            sums[h] = part if sums[h] is None else sums[h] + part
    for a in range(aggregates):
        real, imag = [], []
        for h in range(2):
            top = sums[h][a * 2 * rhs : a * 2 * rhs + rhs]
            low = sums[h][a * 2 * rhs + rhs : (a + 1) * 2 * rhs]
            real.append(top[:, :vectors] + low[:, vectors:])
            imag.append(low[:, :vectors] - top[:, vectors:])
        out_ref[a] = jnp.concatenate(real + imag, axis=1).astype(out_ref.dtype)
    loads[-1].wait()


def restrict(fine, null, operator):
    times, _, _, rhs, sites = fine.shape
    coarse_y = sites // (64 * CZ)
    return pl.pallas_call(
        functools.partial(restrict_kernel, coarse_y),
        in_specs=[pl.BlockSpec(memory_space=pl.ANY)] * 3,
        out_specs=[pl.BlockSpec(memory_space=pltpu.VMEM)] * 3,
        out_shape=[
            pltpu.VMEM((coarse_y * CZ, rhs, 4 * null.shape[3]), jnp.bfloat16),
            pltpu.VMEM(null.shape, null.dtype),
            pltpu.VMEM(operator.shape, operator.dtype),
        ],
        scratch_shapes=[pltpu.VMEM(fine.shape, fine.dtype), pltpu.SemaphoreType.DMA((2 * times + 1,))],
        compiler_params=pltpu.CompilerParams(vmem_limit_bytes=KERNEL_VMEM),
        name="restrict",
    )(in_hbm(fine), in_hbm(null), in_hbm(operator))


def prolong(column, null_ref, out_ref, held, done):
    coarse_y = len(column) // CZ
    times, _, _, rhs, sites = held.shape
    vectors = null_ref.shape[3]
    ids = aggregate_ids((2 * vectors, sites), coarse_y)
    masks = [(lax.rem(ids, CZ) == z).astype(jnp.float32).astype(jnp.bfloat16) for z in range(CZ)]
    rows = aggregate_ids((2 * rhs, sites), coarse_y) // CZ
    mixers = []
    for h in range(2):
        mixer = []
        for y in range(coarse_y):
            real = [column[y * CZ + z][:, h * vectors : (h + 1) * vectors] for z in range(CZ)]
            imag = [column[y * CZ + z][:, (2 + h) * vectors : (3 + h) * vectors] for z in range(CZ)]
            mixer.append(jnp.concatenate([part for z in range(CZ) for part in (real[z], -imag[z])], axis=1))
            mixer.append(jnp.concatenate([part for z in range(CZ) for part in (imag[z], real[z])], axis=1))
        mixers.append(jnp.concatenate(mixer, axis=0))
    copies = []
    for t in range(times):
        for c in range(12):
            null = jnp.concatenate([null_ref[t, 0, c], null_ref[t, 1, c]], axis=0)
            null = jnp.concatenate([null * mask for mask in masks], axis=0)
            every = jnp.dot(mixers[c // 6], null, preferred_element_type=jnp.float32)
            result = every[: 2 * rhs]
            for y in range(1, coarse_y):
                result = jnp.where(rows == y, every[y * 2 * rhs : (y + 1) * 2 * rhs], result)
            result = result.astype(held.dtype)
            held[t, 0, c] = result[:rhs]
            held[t, 1, c] = result[rhs:]
        copies.append(pltpu.make_async_copy(held.at[t], out_ref.at[t], done.at[t]))
        copies[-1].start()
    for copy in copies:
        copy.wait()


def time_sides(even_slice):
    parity = lax.rem(lax.axis_index("zt"), 2)
    if not even_slice:
        parity = 1 - parity
    return 1 + parity, 2 - parity


def for_sites(extent, body):
    for y in range(extent[0]):
        for z in range(extent[1]):
            if extent[2] <= 2:
                for x in range(extent[2]):
                    body((y, z, x))
            else:
                lax.fori_loop(0, extent[2], lambda x, c, y=y, z=z: (body((y, z, x)), c)[1], 0)


def nearby(site, extent):
    found = [site]
    for axis in range(3):
        for step in [1] if extent[axis] == 2 else [1, extent[axis] - 1]:
            moved = site[axis] + step
            moved = lax.rem(moved, extent[axis]) if axis == 2 else moved % extent[axis]
            found.append(site[:axis] + (moved,) + site[axis + 1 :])
    return found


def around(operator, site, extent):
    blocks = [operator[(0, 0) + site]]
    for axis in range(3):
        ahead, behind = operator[(0, 3 + 2 * axis) + site], operator[(0, 4 + 2 * axis) + site]
        if extent[axis] == 2:
            both = ahead.astype(jnp.float32) + behind.astype(jnp.float32)
            blocks.append(both.astype(jnp.bfloat16))
        else:
            blocks += [ahead, behind]
    return list(zip(blocks, nearby(site, extent)))


def products(pairs):
    return lax.dot_general(
        jnp.concatenate([field for _, field in pairs], axis=1),
        jnp.concatenate([block for block, _ in pairs], axis=1),
        LANES,
        preferred_element_type=jnp.float32,
    )


def packed(operator, site, times):
    blocks = [block for block, _ in around(operator, site, operator.shape[2:5])]
    blocks += [operator[(0, d) + site] for d in times]
    return jnp.concatenate([block.T for block in blocks], axis=0)


def packed_stencil(weights, site, here, times):
    extent = weights.shape[:3]
    fields = [here[near] for near in nearby(site, extent)] + [field[site] for field in times]
    depth = len(fields) * weights.shape[4]
    return jnp.dot(jnp.concatenate(fields, axis=1), weights[site][:depth], preferred_element_type=jnp.float32)


def stencil(operator, site, here, times):
    extent = operator.shape[2:5]
    pairs = [(block, here[near]) for block, near in around(operator, site, extent)]
    pairs += [(operator[(0, d) + site], field[site]) for d, field in times]
    return products(pairs)


def relaxed(value, rounded, target, sums):
    image = sums + DIAGONAL_SHIFT * rounded.astype(jnp.float32)
    return value + RELAX_WEIGHT * (target.astype(jnp.float32) - image)


def block_kernel(op_mine, op_pair, block):
    _, odd = time_sides(True)
    _, pair_odd = time_sides(False)
    first = lax.axis_index("zt") < 2

    @pl.when(first)
    def _():
        block[...] = op_pair[0, pair_odd]

    @pl.when(jnp.logical_not(first))
    def _():
        block[...] = op_mine[0, odd]


def gather_kernel(pieces, operator, *refs):
    parts, (rhs_mine, rhs_pair, start_mine, start_pair, message, part_mine) = refs[: 2 * pieces], refs[2 * pieces :]
    extent = operator.shape[2:5]
    position = lax.axis_index("xy")
    even, _ = time_sides(True)
    if pieces > 1:
        parts = (parts[3], parts[1], parts[2], parts[0])
    for whole, held in ((rhs_mine, parts[:pieces]), (rhs_pair, parts[pieces:])):
        for y in range(extent[0]):
            for z in range(extent[1]):
                for x in range(extent[2]):
                    if pieces == 1:
                        whole[y, z, x] = held[0][x, y * extent[1] + z]
                    else:
                        whole[y, z, lax.rem(position + x, pieces)] = held[x][y * extent[1] + z]

    def begin(site):
        start_mine[site] = (RELAX_WEIGHT * rhs_mine[site].astype(jnp.float32)).astype(jnp.bfloat16)
        message[(0,) + site] = start_mine[site]
        start_pair[site] = (RELAX_WEIGHT * rhs_pair[site].astype(jnp.float32)).astype(jnp.bfloat16)

    for_sites(extent, begin)
    here = start_mine

    def step(site):
        sums = stencil(operator, site, here, [(even, start_pair)])
        value = RELAX_WEIGHT * rhs_mine[site].astype(jnp.float32)
        part = relaxed(value, here[site], rhs_mine[site], sums)
        part_mine[site] = part
        message[(1,) + site] = part.astype(jnp.bfloat16)

    for_sites(extent, step)


def first_pair_kernel(op_mine, op_pair, rhs_pair, here, other, part_pair, packed_mine, packed_pair, through_pair):
    sides, pair_sides = time_sides(True), time_sides(False)

    def step(site):
        packed_mine[site] = packed(op_mine, site, sides)
        packed_pair[site] = packed(op_pair, site, pair_sides)
        sums = packed_stencil(packed_pair, site, here, [other])
        value = RELAX_WEIGHT * rhs_pair[site].astype(jnp.float32)
        part_pair[site] = relaxed(value, here[site], rhs_pair[site], sums).astype(jnp.bfloat16)
        outer, inner = packed_pair[site][side_rows(packed_pair, 1)], packed_mine[site][side_rows(packed_mine, 2)]
        through_pair[site] = two_steps(outer, inner).astype(jnp.bfloat16)

    for_sites(op_mine.shape[2:5], step)


def second_pair_kernel(
    op_mine, op_pair, back_near, rhs_mine, rhs_pair, here, other, sent, part_mine, rest, through_near, part_pair, returned,
):
    extent = op_mine.shape[:3]
    columns = op_mine.shape[4]
    mine = sent.at[1]

    def first(site):
        sums = packed_stencil(op_pair, site, here, [other])
        part_pair[site] = relaxed(here[site].astype(jnp.float32), here[site], rhs_pair[site], sums).astype(jnp.bfloat16)
        value = -RELAX_WEIGHT * products([(back_near[site], other[site])])
        returned[site] = value.astype(jnp.bfloat16)

    for_sites(extent, first)

    def second(site):
        sums = packed_stencil(op_mine, site, mine, [part_pair, returned])
        rest[site] = relaxed(part_mine[site], mine[site], rhs_mine[site], sums)
        for index, near in enumerate(nearby(site, extent)):
            side = op_mine[near][side_rows(op_mine, 1)]
            block = two_steps(side, op_mine[site][index * columns : (index + 1) * columns])
            if index == 0:
                kept = RELAX_WEIGHT * (1 - RELAX_WEIGHT * DIAGONAL_SHIFT)
                block = block - kept * side.astype(jnp.float32)
            through_near[site + (slice(index * columns, (index + 1) * columns),)] = block.astype(jnp.bfloat16)

    for_sites(extent, second)


def two_steps(first, second):
    return RELAX_WEIGHT * RELAX_WEIGHT * jnp.dot(first, second, preferred_element_type=jnp.float32)


def second_near_kernel(op_mine, back_near, rhs_mine, sent, part_mine, part_pair, near, rest, one_mine, one_near):
    def first(site):
        value = near_step(op_mine, part_mine, near.at[0], site)
        rest[site] = value
        one_mine[site] = value.astype(jnp.bfloat16)
        one_near[site] = return_step(back_near, sent, near, site)

    for_sites(op_mine.shape[:3], first)

    def second(site):
        sums = packed_stencil(op_mine, site, one_mine, [part_pair, one_near])
        rest[site] = relaxed(rest[site], one_mine[site], rhs_mine[site], sums)

    for_sites(op_mine.shape[:3], second)


def second_far_kernel(through_pair, far, rest, field_mine, value_mine):
    def step(site):
        value = rest[site] + jnp.dot(far[site], through_pair[site], preferred_element_type=jnp.float32)
        value_mine[site] = value
        field_mine[site] = value.astype(jnp.bfloat16)

    for_sites(rest.shape[:3], step)


def side_rows(weights, last):
    depth, columns = weights.shape[3:]
    return slice(depth - last * columns, depth - (last - 1) * columns)


def side_product(field, weights, site, last):
    return jnp.dot(field[site], weights[site][side_rows(weights, last)], preferred_element_type=jnp.float32)


def near_step(weights, part, received, site):
    return part[site] - RELAX_WEIGHT * side_product(received, weights, site, 1)


def return_step(back_near, sent, near, site):
    value = near[(1,) + site].astype(jnp.float32) - RELAX_WEIGHT * products([(back_near[site], sent[(0,) + site])])
    return value.astype(jnp.bfloat16)


def third_own_kernel(op_mine, rhs_mine, field_mine, value_mine, rest):
    def step(site):
        sums = packed_stencil(op_mine, site, field_mine, [])
        rest[site] = relaxed(value_mine[site], field_mine[site], rhs_mine[site], sums)

    for_sites(op_mine.shape[:3], step)


def third_kernel(op_mine, rest, field_mine, field_pair, message, part_next):
    def step(site):
        part = rest[site] - RELAX_WEIGHT * side_product(field_pair, op_mine, site, 2)
        part_next[site] = part
        message[(0,) + site] = field_mine[site]
        message[(1,) + site] = part.astype(jnp.bfloat16)

    for_sites(op_mine.shape[:3], step)


def last_kernel(
    op_mine, through_near, through_pair, rest, near, far, null,
    fine_out, coarse_out, result, held, done,
):
    extent = rest.shape[:3]
    field = near.at[0]

    def step(site):
        sums = jnp.dot(
            jnp.concatenate([field[other] for other in nearby(site, extent)], axis=1),
            through_near[site],
            preferred_element_type=jnp.float32,
        )
        sums += jnp.dot(far[site], through_pair[site], preferred_element_type=jnp.float32)
        value = rest[site] + sums - RELAX_WEIGHT * jnp.dot(
            near[(1,) + site], op_mine[site][side_rows(op_mine, 1)], preferred_element_type=jnp.float32
        )
        result[(0,) + site] = value.astype(jnp.bfloat16)

    for_sites(extent, step)
    times = held.shape[0]
    copy = pltpu.make_async_copy(result, coarse_out, done.at[times])
    copy.start()
    position = lax.axis_index("xy")
    column = [result[0, y, z, position] for y in range(extent[0]) for z in range(extent[1])]
    prolong(column, null, fine_out, held, done)
    copy.wait()


def last(shape, *operands):
    full, times = operands[3].shape, shape[0]
    return pl.pallas_call(
        last_kernel,
        in_specs=[pl.BlockSpec(memory_space=pltpu.VMEM)] * len(operands),
        out_specs=[pl.BlockSpec(memory_space=pl.ANY)] * 2,
        out_shape=[
            jax.ShapeDtypeStruct(shape, jnp.bfloat16),
            jax.ShapeDtypeStruct((1,) + full, jnp.bfloat16),
        ],
        scratch_shapes=[
            pltpu.VMEM((1,) + full, jnp.bfloat16),
            pltpu.VMEM(shape, jnp.bfloat16),
            pltpu.SemaphoreType.DMA((times + 1,)),
        ],
        compiler_params=pltpu.CompilerParams(vmem_limit_bytes=KERNEL_VMEM),
        name="last",
    )(*[in_vmem(operand) for operand in operands])


def packed_depth(operator):
    blocks = 3 + sum(1 if length == 2 else 2 for length in operator.shape[2:5])
    return blocks * operator.shape[6]


def in_hbm(array):
    return pltpu.with_memory_space_constraint(array, pltpu.HBM)


def in_vmem(array):
    return pltpu.with_memory_space_constraint(array, pltpu.VMEM)


def kernel_call(kernel, name, outs, scratch, *operands, flops=0):
    return pl.pallas_call(
        kernel,
        in_specs=[pl.BlockSpec(memory_space=pltpu.VMEM)] * len(operands),
        out_specs=[pl.BlockSpec(memory_space=pltpu.VMEM)] * len(outs),
        out_shape=[pltpu.VMEM(shape, dtype) for shape, dtype in outs],
        scratch_shapes=[pltpu.VMEM(shape, dtype) for shape, dtype in scratch],
        compiler_params=pltpu.CompilerParams(vmem_limit_bytes=KERNEL_VMEM),
        cost_estimate=pl.CostEstimate(flops=flops, bytes_accessed=0, transcendentals=0) if flops else None,
        name=name,
    )(*[in_vmem(operand) for operand in operands])


def exchange_plan():
    slices, columns = lax.axis_size("zt"), lax.axis_size("xy")
    other = [i ^ 1 for i in range(slices)]
    across = [(i + 1 if i % 2 else i - 1) % slices for i in range(slices)]

    def permutation(target, turn=0):
        return [
            (i * columns + j, target[i] * columns + (j + turn) % columns) for i in range(slices) for j in range(columns)
        ]

    def send(array, target, turn=0):
        return lax.ppermute(array, ("zt", "xy"), permutation(target, turn))

    far = [other[across[i]] for i in range(slices)]
    return send, list(range(slices)), other, across, far


def per_device(fine_vectors, null_vectors, coarse_operator):
    send, same, other, across, far = exchange_plan()
    columns = lax.axis_size("xy")
    extent = coarse_operator.shape[2:5]
    bf16, f32 = jnp.bfloat16, jnp.float32
    own, null_kept, operator = restrict(fine_vectors, null_vectors, coarse_operator)
    full = extent + own.shape[1:]
    if columns == 2:
        corner, pair, beside = send(own, other, 1), send(own, other), send(own, same, 1)
        parts = [corner, beside, pair, own]
    else:
        every = lax.all_gather(own, "xy")
        parts = [every, send(every, other)]
    op_pair = send(coarse_operator, other)
    (block,) = kernel_call(block_kernel, "block", [(operator.shape[2:], bf16)], [], operator, op_pair)
    back_near = send(block, [across[1], across[0]] + across[2:])
    rhs_mine, rhs_pair, start_mine, start_pair, sent, part_mine = kernel_call(
        functools.partial(gather_kernel, len(parts) // 2),
        "gather",
        [(full, bf16)] * 4 + [((2,) + full, bf16), (full, f32)],
        [],
        operator,
        *parts,
        flops=GATHER_FLOPS,
    )
    near_message, far_field = send(sent, across), send(start_mine, far)
    packed_shape = extent + (packed_depth(operator), operator.shape[6])
    part_pair, packed_mine, packed_pair, through_pair = kernel_call(
        first_pair_kernel,
        "pair_one",
        [(full, bf16), (packed_shape, bf16), (packed_shape, bf16), (operator.shape[2:], bf16)],
        [],
        operator, op_pair, rhs_pair, start_pair, start_mine,
    )
    (rest,) = kernel_call(
        second_near_kernel, "second_near", [(full, f32)], [(full, bf16)] * 2,
        packed_mine, back_near, rhs_mine, sent, part_mine, part_pair, near_message,
    )
    field_mine, value_mine = kernel_call(
        second_far_kernel, "second_far", [(full, bf16), (full, f32)], [], through_pair, far_field, rest,
    )
    field_pair = send(field_mine, other)
    (rest,) = kernel_call(
        third_own_kernel, "third_own", [(full, f32)], [], packed_mine, rhs_mine, field_mine, value_mine,
    )
    sent, part_mine = kernel_call(
        third_kernel, "third", [((2,) + full, bf16), (full, f32)], [], packed_mine, rest, field_mine, field_pair,
    )
    near_message, far_field = send(sent, across), send(field_mine, far)
    rest, through_near = kernel_call(
        second_pair_kernel,
        "pair_two",
        [(full, f32), (extent + (packed_shape[3] - 2 * packed_shape[4], packed_shape[4]), bf16)],
        [(full, bf16)] * 2,
        packed_mine, packed_pair, back_near, rhs_mine, rhs_pair, field_pair, field_mine, sent, part_mine,
    )
    fine_correction, coarse_iterate = last(
        fine_vectors.shape,
        packed_mine, through_near, through_pair, rest, near_message, far_field, null_kept,
    )
    return (fine_correction, coarse_iterate)


def solution(mesh):
    return jax.shard_map(
        per_device,
        mesh=mesh,
        in_specs=(
            P("zt", None, None, None, "xy"),
            P("zt", None, None, None, "xy"),
            P("zt", None, None, None, None, None, None),
        ),
        out_specs=(P("zt", None, None, None, "xy"), P("zt", None, None, None, None, None)),
        check_vma=False,
    )
```

```python
import functools

import jax
import jax.numpy as jnp
from jax import lax
from jax.experimental import pallas as pl
from jax.experimental.pallas import tpu as pltpu
from jax.sharding import PartitionSpec as P

CZ = 2
APPLIES = 4
RELAX_WEIGHT = 0.3
DIAGONAL_SHIFT = 3.0
LANES = (((1,), (1,)), ((), ()))
KERNEL_VMEM = 16 * 1024 * 1024
GATHER_FLOPS = 10**10


def aggregate_ids(shape, coarse_y):
    site = lax.broadcasted_iota(jnp.int32, shape, len(shape) - 1)
    row = 4 * coarse_y
    y = lax.rem(site, row) // 4
    z = lax.rem(site, row * 4 * CZ) // (row * 4)
    return y * CZ + z


def restrict_kernel(coarse_y, fine_hbm, null_hbm, operator_hbm, out_ref, null_ref, operator, fine_ref, loaded):
    aggregates = coarse_y * CZ
    times, _, _, rhs, sites = fine_ref.shape
    vectors = null_ref.shape[3]
    loads = []
    for t in range(times):
        loads.append(pltpu.make_async_copy(fine_hbm.at[t], fine_ref.at[t], loaded.at[2 * t]))
        loads.append(pltpu.make_async_copy(null_hbm.at[t], null_ref.at[t], loaded.at[2 * t + 1]))
    loads.append(pltpu.make_async_copy(operator_hbm, operator, loaded.at[2 * times]))
    for load in loads:
        load.start()
    ids = aggregate_ids((2 * rhs, sites), coarse_y)
    masks = [(ids == a).astype(jnp.float32).astype(jnp.bfloat16) for a in range(aggregates)]
    sums = [None, None]
    for t in range(times):
        loads[2 * t].wait()
        loads[2 * t + 1].wait()
        for h in range(2):
            left, right = [], []
            for c in range(h * 6, h * 6 + 6):
                fine = jnp.concatenate([fine_ref[t, 0, c], fine_ref[t, 1, c]], axis=0)
                left.append(jnp.concatenate([fine * m for m in masks], axis=0))
                right.append(jnp.concatenate([null_ref[t, 0, c], null_ref[t, 1, c]], axis=0))
            part = lax.dot_general(
                jnp.concatenate(left, axis=1),
                jnp.concatenate(right, axis=1),
                LANES,
                preferred_element_type=jnp.float32,
            )
            sums[h] = part if sums[h] is None else sums[h] + part
    for a in range(aggregates):
        real, imag = [], []
        for h in range(2):
            top = sums[h][a * 2 * rhs : a * 2 * rhs + rhs]
            low = sums[h][a * 2 * rhs + rhs : (a + 1) * 2 * rhs]
            real.append(top[:, :vectors] + low[:, vectors:])
            imag.append(low[:, :vectors] - top[:, vectors:])
        out_ref[a] = jnp.concatenate(real + imag, axis=1).astype(out_ref.dtype)
    loads[-1].wait()


def restrict(fine, null, operator):
    times, _, _, rhs, sites = fine.shape
    coarse_y = sites // (64 * CZ)
    return pl.pallas_call(
        functools.partial(restrict_kernel, coarse_y),
        in_specs=[pl.BlockSpec(memory_space=pl.ANY)] * 3,
        out_specs=[pl.BlockSpec(memory_space=pltpu.VMEM)] * 3,
        out_shape=[
            pltpu.VMEM((coarse_y * CZ, rhs, 4 * null.shape[3]), jnp.bfloat16),
            pltpu.VMEM(null.shape, null.dtype),
            pltpu.VMEM(operator.shape, operator.dtype),
        ],
        scratch_shapes=[pltpu.VMEM(fine.shape, fine.dtype), pltpu.SemaphoreType.DMA((2 * times + 1,))],
        compiler_params=pltpu.CompilerParams(vmem_limit_bytes=KERNEL_VMEM),
        name="restrict",
    )(in_hbm(fine), in_hbm(null), in_hbm(operator))


def prolong(column, null_ref, out_ref, held, done):
    coarse_y = len(column) // CZ
    times, _, _, rhs, sites = held.shape
    vectors = null_ref.shape[3]
    ids = aggregate_ids((2 * vectors, sites), coarse_y)
    masks = [(lax.rem(ids, CZ) == z).astype(jnp.float32).astype(jnp.bfloat16) for z in range(CZ)]
    rows = aggregate_ids((2 * rhs, sites), coarse_y) // CZ
    mixers = []
    for h in range(2):
        mixer = []
        for y in range(coarse_y):
            real = [column[y * CZ + z][:, h * vectors : (h + 1) * vectors] for z in range(CZ)]
            imag = [column[y * CZ + z][:, (2 + h) * vectors : (3 + h) * vectors] for z in range(CZ)]
            mixer.append(jnp.concatenate([part for z in range(CZ) for part in (real[z], -imag[z])], axis=1))
            mixer.append(jnp.concatenate([part for z in range(CZ) for part in (imag[z], real[z])], axis=1))
        mixers.append(jnp.concatenate(mixer, axis=0))
    copies = []
    for t in range(times):
        for c in range(12):
            null = jnp.concatenate([null_ref[t, 0, c], null_ref[t, 1, c]], axis=0)
            null = jnp.concatenate([null * mask for mask in masks], axis=0)
            every = jnp.dot(mixers[c // 6], null, preferred_element_type=jnp.float32)
            result = every[: 2 * rhs]
            for y in range(1, coarse_y):
                result = jnp.where(rows == y, every[y * 2 * rhs : (y + 1) * 2 * rhs], result)
            result = result.astype(held.dtype)
            held[t, 0, c] = result[:rhs]
            held[t, 1, c] = result[rhs:]
        copies.append(pltpu.make_async_copy(held.at[t], out_ref.at[t], done.at[t]))
        copies[-1].start()
    for copy in copies:
        copy.wait()


def time_sides(even_slice):
    parity = lax.rem(lax.axis_index("zt"), 2)
    if not even_slice:
        parity = 1 - parity
    return 1 + parity, 2 - parity


def for_sites(extent, body):
    for y in range(extent[0]):
        for z in range(extent[1]):
            if extent[2] <= 2:
                for x in range(extent[2]):
                    body((y, z, x))
            else:
                lax.fori_loop(0, extent[2], lambda x, c, y=y, z=z: (body((y, z, x)), c)[1], 0)


def nearby(site, extent):
    found = [site]
    for axis in range(3):
        for step in [1] if extent[axis] == 2 else [1, extent[axis] - 1]:
            moved = site[axis] + step
            moved = lax.rem(moved, extent[axis]) if axis == 2 else moved % extent[axis]
            found.append(site[:axis] + (moved,) + site[axis + 1 :])
    return found


def around(operator, site, extent):
    blocks = [operator[(0, 0) + site]]
    for axis in range(3):
        ahead, behind = operator[(0, 3 + 2 * axis) + site], operator[(0, 4 + 2 * axis) + site]
        if extent[axis] == 2:
            both = ahead.astype(jnp.float32) + behind.astype(jnp.float32)
            blocks.append(both.astype(jnp.bfloat16))
        else:
            blocks += [ahead, behind]
    return list(zip(blocks, nearby(site, extent)))


def products(pairs):
    return lax.dot_general(
        jnp.concatenate([field for _, field in pairs], axis=1),
        jnp.concatenate([block for block, _ in pairs], axis=1),
        LANES,
        preferred_element_type=jnp.float32,
    )


def packed(operator, site, times):
    blocks = [block for block, _ in around(operator, site, operator.shape[2:5])]
    blocks += [operator[(0, d) + site] for d in times]
    return jnp.concatenate([block.T for block in blocks], axis=0)


def packed_stencil(weights, site, here, times):
    extent = weights.shape[:3]
    fields = [here[near] for near in nearby(site, extent)] + [field[site] for field in times]
    depth = len(fields) * weights.shape[4]
    return jnp.dot(jnp.concatenate(fields, axis=1), weights[site][:depth], preferred_element_type=jnp.float32)


def stencil(operator, site, here, times):
    extent = operator.shape[2:5]
    pairs = [(block, here[near]) for block, near in around(operator, site, extent)]
    pairs += [(operator[(0, d) + site], field[site]) for d, field in times]
    return products(pairs)


def relaxed(value, rounded, target, sums):
    image = sums + DIAGONAL_SHIFT * rounded.astype(jnp.float32)
    return value + RELAX_WEIGHT * (target.astype(jnp.float32) - image)


def block_kernel(op_mine, op_pair, block):
    _, odd = time_sides(True)
    _, pair_odd = time_sides(False)
    first = lax.axis_index("zt") < 2

    @pl.when(first)
    def _():
        block[...] = op_pair[0, pair_odd]

    @pl.when(jnp.logical_not(first))
    def _():
        block[...] = op_mine[0, odd]


def gather_kernel(pieces, operator, *refs):
    parts, (rhs_mine, rhs_pair, start_mine, start_pair, message, part_mine) = refs[: 2 * pieces], refs[2 * pieces :]
    extent = operator.shape[2:5]
    position = lax.axis_index("xy")
    even, _ = time_sides(True)
    if pieces > 1:
        parts = (parts[3], parts[1], parts[2], parts[0])
    for whole, held in ((rhs_mine, parts[:pieces]), (rhs_pair, parts[pieces:])):
        for y in range(extent[0]):
            for z in range(extent[1]):
                for x in range(extent[2]):
                    if pieces == 1:
                        whole[y, z, x] = held[0][x, y * extent[1] + z]
                    else:
                        whole[y, z, lax.rem(position + x, pieces)] = held[x][y * extent[1] + z]

    def begin(site):
        start_mine[site] = (RELAX_WEIGHT * rhs_mine[site].astype(jnp.float32)).astype(jnp.bfloat16)
        message[(0,) + site] = start_mine[site]
        start_pair[site] = (RELAX_WEIGHT * rhs_pair[site].astype(jnp.float32)).astype(jnp.bfloat16)

    for_sites(extent, begin)
    here = start_mine

    def step(site):
        sums = stencil(operator, site, here, [(even, start_pair)])
        value = RELAX_WEIGHT * rhs_mine[site].astype(jnp.float32)
        part = relaxed(value, here[site], rhs_mine[site], sums)
        part_mine[site] = part
        message[(1,) + site] = part.astype(jnp.bfloat16)

    for_sites(extent, step)


def first_pair_kernel(
    op_mine, op_pair, rhs_mine, rhs_pair, here, other, sent, part_mine,
    packed_mine, packed_pair, rest, through_near, through_pair, through_mine, part_pair,
):
    sides, pair_sides = time_sides(True), time_sides(False)

    def step(site):
        packed_mine[site] = packed(op_mine, site, sides)
        packed_pair[site] = packed(op_pair, site, pair_sides)
        sums = packed_stencil(packed_pair, site, here, [other])
        value = RELAX_WEIGHT * rhs_pair[site].astype(jnp.float32)
        part_pair[site] = relaxed(value, here[site], rhs_pair[site], sums).astype(jnp.bfloat16)
        outer, inner = packed_pair[site][side_rows(packed_pair, 1)], packed_mine[site][side_rows(packed_mine, 2)]
        through_pair[site] = two_steps(outer, inner).astype(jnp.bfloat16)
        outer, inner = packed_mine[site][side_rows(packed_mine, 1)], packed_pair[site][side_rows(packed_pair, 2)]
        through_mine[site] = two_steps(outer, inner).astype(jnp.bfloat16)

    extent = op_mine.shape[2:5]
    columns = op_mine.shape[6]
    mine = sent.at[1]
    for_sites(extent, step)

    def ahead(site):
        sums = packed_stencil(packed_mine, site, mine, [part_pair])
        rest[site] = relaxed(part_mine[site], mine[site], rhs_mine[site], sums)
        for index, near in enumerate(nearby(site, extent)):
            side = packed_mine[near][side_rows(packed_mine, 1)]
            block = two_steps(side, packed_mine[site][index * columns : (index + 1) * columns])
            if index == 0:
                kept = RELAX_WEIGHT * (1 - RELAX_WEIGHT * DIAGONAL_SHIFT)
                block = block - kept * side.astype(jnp.float32)
            through_near[site + (slice(index * columns, (index + 1) * columns),)] = block.astype(jnp.bfloat16)

    for_sites(extent, ahead)


def second_pair_kernel(
    op_mine, op_pair, back_near, rhs_mine, rhs_pair, here, other, sent, part_mine, rest, part_pair, returned,
):
    extent = op_mine.shape[:3]
    mine = sent.at[1]

    def first(site):
        sums = packed_stencil(op_pair, site, here, [other])
        part_pair[site] = relaxed(here[site].astype(jnp.float32), here[site], rhs_pair[site], sums).astype(jnp.bfloat16)
        value = -RELAX_WEIGHT * products([(back_near[site], other[site])])
        returned[site] = value.astype(jnp.bfloat16)

    for_sites(extent, first)

    def second(site):
        sums = packed_stencil(op_mine, site, mine, [part_pair, returned])
        rest[site] = relaxed(part_mine[site], mine[site], rhs_mine[site], sums)

    for_sites(extent, second)


def two_steps(first, second):
    return RELAX_WEIGHT * RELAX_WEIGHT * jnp.dot(first, second, preferred_element_type=jnp.float32)


def second_kernel(op_mine, through_near, through_mine, back_near, sent, rest, near, value, swapped, one_near):
    extent = rest.shape[:3]
    field = near.at[0]

    def first(site):
        sums = products([(back_near[site], sent[(0,) + site])])
        one_near[site] = (near[(1,) + site].astype(jnp.float32) - RELAX_WEIGHT * sums).astype(jnp.bfloat16)
        sums = jnp.dot(field[site], through_mine[site], preferred_element_type=jnp.float32)
        swapped[(1,) + site] = sums.astype(jnp.bfloat16)

    for_sites(extent, first)

    def second(site):
        result = rest[site] + answer(op_mine, through_near, field, one_near, site)
        value[site] = result
        swapped[(0,) + site] = result.astype(jnp.bfloat16)

    for_sites(extent, second)


def answer(op_mine, through_near, field, one_near, site):
    fields = [field[other] for other in nearby(site, through_near.shape[:3])]
    sums = jnp.dot(jnp.concatenate(fields, axis=1), through_near[site], preferred_element_type=jnp.float32)
    return sums - RELAX_WEIGHT * side_product(one_near, op_mine, site, 1)


def side_rows(weights, last):
    depth, columns = weights.shape[3:]
    return slice(depth - last * columns, depth - (last - 1) * columns)


def side_product(field, weights, site, last):
    return jnp.dot(field[site], weights[site][side_rows(weights, last)], preferred_element_type=jnp.float32)


def third_own_kernel(op_mine, rhs_mine, swapped, value, rest):
    field = swapped.at[0]

    def step(site):
        sums = packed_stencil(op_mine, site, field, [])
        rest[site] = relaxed(value[site], field[site], rhs_mine[site], sums)

    for_sites(op_mine.shape[:3], step)


def third_kernel(op_mine, rest, value, swapped, received, message, field_mine, field_pair, part_next):
    late = received.at[1]

    def first(site):
        field = received[(0,) + site].astype(jnp.float32) + swapped[(1,) + site].astype(jnp.float32)
        field_pair[site] = field.astype(jnp.bfloat16)
        field = (value[site] + late[site].astype(jnp.float32)).astype(jnp.bfloat16)
        field_mine[site] = field
        message[(0,) + site] = field

    for_sites(op_mine.shape[:3], first)

    def second(site):
        sums = packed_stencil(op_mine, site, late, [field_pair])
        kept = (1 - RELAX_WEIGHT * DIAGONAL_SHIFT) * late[site].astype(jnp.float32)
        part = rest[site] + kept - RELAX_WEIGHT * sums
        part_next[site] = part
        message[(1,) + site] = part.astype(jnp.bfloat16)

    for_sites(op_mine.shape[:3], second)


def last_kernel(
    op_mine, through_near, through_pair, rest, near, far, null,
    fine_out, coarse_out, result, held, done,
):
    extent = rest.shape[:3]
    field, part = near.at[0], near.at[1]

    def step(site):
        value = rest[site] + answer(op_mine, through_near, field, part, site)
        value += jnp.dot(far[site], through_pair[site], preferred_element_type=jnp.float32)
        result[(0,) + site] = value.astype(jnp.bfloat16)

    for_sites(extent, step)
    times = held.shape[0]
    copy = pltpu.make_async_copy(result, coarse_out, done.at[times])
    copy.start()
    position = lax.axis_index("xy")
    column = [result[0, y, z, position] for y in range(extent[0]) for z in range(extent[1])]
    prolong(column, null, fine_out, held, done)
    copy.wait()


def last(shape, *operands):
    full, times = operands[3].shape, shape[0]
    return pl.pallas_call(
        last_kernel,
        in_specs=[pl.BlockSpec(memory_space=pltpu.VMEM)] * len(operands),
        out_specs=[pl.BlockSpec(memory_space=pl.ANY)] * 2,
        out_shape=[
            jax.ShapeDtypeStruct(shape, jnp.bfloat16),
            jax.ShapeDtypeStruct((1,) + full, jnp.bfloat16),
        ],
        scratch_shapes=[
            pltpu.VMEM((1,) + full, jnp.bfloat16),
            pltpu.VMEM(shape, jnp.bfloat16),
            pltpu.SemaphoreType.DMA((times + 1,)),
        ],
        compiler_params=pltpu.CompilerParams(vmem_limit_bytes=KERNEL_VMEM),
        name="last",
    )(*[in_vmem(operand) for operand in operands])


def packed_depth(operator):
    blocks = 3 + sum(1 if length == 2 else 2 for length in operator.shape[2:5])
    return blocks * operator.shape[6]


def in_hbm(array):
    return pltpu.with_memory_space_constraint(array, pltpu.HBM)


def in_vmem(array):
    return pltpu.with_memory_space_constraint(array, pltpu.VMEM)


def kernel_call(kernel, name, outs, scratch, *operands, flops=0):
    return pl.pallas_call(
        kernel,
        in_specs=[pl.BlockSpec(memory_space=pltpu.VMEM)] * len(operands),
        out_specs=[pl.BlockSpec(memory_space=pltpu.VMEM)] * len(outs),
        out_shape=[pltpu.VMEM(shape, dtype) for shape, dtype in outs],
        scratch_shapes=[pltpu.VMEM(shape, dtype) for shape, dtype in scratch],
        compiler_params=pltpu.CompilerParams(vmem_limit_bytes=KERNEL_VMEM),
        cost_estimate=pl.CostEstimate(flops=flops, bytes_accessed=0, transcendentals=0) if flops else None,
        name=name,
    )(*[in_vmem(operand) for operand in operands])


def exchange_plan():
    slices, columns = lax.axis_size("zt"), lax.axis_size("xy")
    other = [i ^ 1 for i in range(slices)]
    across = [(i + 1 if i % 2 else i - 1) % slices for i in range(slices)]

    def permutation(target, turn=0):
        return [
            (i * columns + j, target[i] * columns + (j + turn) % columns) for i in range(slices) for j in range(columns)
        ]

    def send(array, target, turn=0):
        return lax.ppermute(array, ("zt", "xy"), permutation(target, turn))

    far = [other[across[i]] for i in range(slices)]
    return send, list(range(slices)), other, across, far


def per_device(fine_vectors, null_vectors, coarse_operator):
    send, same, other, across, far = exchange_plan()
    columns = lax.axis_size("xy")
    extent = coarse_operator.shape[2:5]
    bf16, f32 = jnp.bfloat16, jnp.float32
    own, null_kept, operator = restrict(fine_vectors, null_vectors, coarse_operator)
    full = extent + own.shape[1:]
    if columns == 2:
        corner, pair, beside = send(own, other, 1), send(own, other), send(own, same, 1)
        parts = [corner, beside, pair, own]
    else:
        every = lax.all_gather(own, "xy")
        parts = [every, send(every, other)]
    op_pair = send(coarse_operator, other)
    (block,) = kernel_call(block_kernel, "block", [(operator.shape[2:], bf16)], [], operator, op_pair)
    back_near = send(block, [across[1], across[0]] + across[2:])
    rhs_mine, rhs_pair, start_mine, start_pair, sent, part_mine = kernel_call(
        functools.partial(gather_kernel, len(parts) // 2),
        "gather",
        [(full, bf16)] * 4 + [((2,) + full, bf16), (full, f32)],
        [],
        operator,
        *parts,
        flops=GATHER_FLOPS,
    )
    near_message = send(sent, across)
    packed_shape = extent + (packed_depth(operator), operator.shape[6])
    near_shape = extent + (packed_shape[3] - 2 * packed_shape[4], packed_shape[4])
    packed_mine, packed_pair, rest, through_near, through_pair, through_mine = kernel_call(
        first_pair_kernel,
        "pair_one",
        [(packed_shape, bf16), (packed_shape, bf16), (full, f32), (near_shape, bf16)] + [(operator.shape[2:], bf16)] * 2,
        [(full, bf16)],
        operator, op_pair, rhs_mine, rhs_pair, start_pair, start_mine, sent, part_mine,
    )
    value, swapped = kernel_call(
        second_kernel, "second", [(full, f32), ((2,) + full, bf16)], [(full, bf16)],
        packed_mine, through_near, through_mine, back_near, sent, rest, near_message,
    )
    received = send(swapped, other)
    (rest,) = kernel_call(
        third_own_kernel, "third_own", [(full, f32)], [], packed_mine, rhs_mine, swapped, value,
    )
    sent, field_mine, field_pair, part_mine = kernel_call(
        third_kernel, "third", [((2,) + full, bf16), (full, bf16), (full, bf16), (full, f32)], [],
        packed_mine, rest, value, swapped, received,
    )
    near_message, far_field = send(sent, across), send(field_mine, far)
    (rest,) = kernel_call(
        second_pair_kernel, "pair_two", [(full, f32)], [(full, bf16)] * 2,
        packed_mine, packed_pair, back_near, rhs_mine, rhs_pair, field_pair, field_mine, sent, part_mine,
    )
    fine_correction, coarse_iterate = last(
        fine_vectors.shape,
        packed_mine, through_near, through_pair, rest, near_message, far_field, null_kept,
    )
    return (fine_correction, coarse_iterate)


def solution(mesh):
    return jax.shard_map(
        per_device,
        mesh=mesh,
        in_specs=(
            P("zt", None, None, None, "xy"),
            P("zt", None, None, None, "xy"),
            P("zt", None, None, None, None, None, None),
        ),
        out_specs=(P("zt", None, None, None, "xy"), P("zt", None, None, None, None, None)),
        check_vma=False,
    )
```

```python
import functools

import jax
import jax.numpy as jnp
from jax import lax
from jax.experimental import pallas as pl
from jax.experimental.pallas import tpu as pltpu
from jax.sharding import PartitionSpec as P

CZ = 2
APPLIES = 4
RELAX_WEIGHT = 0.3
DIAGONAL_SHIFT = 3.0
LANES = (((1,), (1,)), ((), ()))
KERNEL_VMEM = 16 * 1024 * 1024
GATHER_FLOPS = 10**10


def aggregate_ids(shape, coarse_y):
    site = lax.broadcasted_iota(jnp.int32, shape, len(shape) - 1)
    row = 4 * coarse_y
    y = lax.rem(site, row) // 4
    z = lax.rem(site, row * 4 * CZ) // (row * 4)
    return y * CZ + z


def restrict_kernel(coarse_y, fine_hbm, null_hbm, operator_hbm, out_ref, null_ref, operator, fine_ref, loaded):
    aggregates = coarse_y * CZ
    times, _, _, rhs, sites = fine_ref.shape
    vectors = null_ref.shape[3]
    loads = []
    for t in range(times):
        loads.append(pltpu.make_async_copy(fine_hbm.at[t], fine_ref.at[t], loaded.at[2 * t]))
        loads.append(pltpu.make_async_copy(null_hbm.at[t], null_ref.at[t], loaded.at[2 * t + 1]))
    loads.append(pltpu.make_async_copy(operator_hbm, operator, loaded.at[2 * times]))
    for load in loads:
        load.start()
    ids = aggregate_ids((2 * rhs, sites), coarse_y)
    masks = [(ids == a).astype(jnp.float32).astype(jnp.bfloat16) for a in range(aggregates)]
    sums = [None, None]
    for t in range(times):
        loads[2 * t].wait()
        loads[2 * t + 1].wait()
        for h in range(2):
            left, right = [], []
            for c in range(h * 6, h * 6 + 6):
                fine = jnp.concatenate([fine_ref[t, 0, c], fine_ref[t, 1, c]], axis=0)
                left.append(jnp.concatenate([fine * m for m in masks], axis=0))
                right.append(jnp.concatenate([null_ref[t, 0, c], null_ref[t, 1, c]], axis=0))
            part = lax.dot_general(
                jnp.concatenate(left, axis=1),
                jnp.concatenate(right, axis=1),
                LANES,
                preferred_element_type=jnp.float32,
            )
            sums[h] = part if sums[h] is None else sums[h] + part
    for a in range(aggregates):
        real, imag = [], []
        for h in range(2):
            top = sums[h][a * 2 * rhs : a * 2 * rhs + rhs]
            low = sums[h][a * 2 * rhs + rhs : (a + 1) * 2 * rhs]
            real.append(top[:, :vectors] + low[:, vectors:])
            imag.append(low[:, :vectors] - top[:, vectors:])
        out_ref[a] = jnp.concatenate(real + imag, axis=1).astype(out_ref.dtype)
    loads[-1].wait()


def restrict(fine, null, operator):
    times, _, _, rhs, sites = fine.shape
    coarse_y = sites // (64 * CZ)
    return pl.pallas_call(
        functools.partial(restrict_kernel, coarse_y),
        in_specs=[pl.BlockSpec(memory_space=pl.ANY)] * 3,
        out_specs=[pl.BlockSpec(memory_space=pltpu.VMEM)] * 3,
        out_shape=[
            pltpu.VMEM((coarse_y * CZ, rhs, 4 * null.shape[3]), jnp.bfloat16),
            pltpu.VMEM(null.shape, null.dtype),
            pltpu.VMEM(operator.shape, operator.dtype),
        ],
        scratch_shapes=[pltpu.VMEM(fine.shape, fine.dtype), pltpu.SemaphoreType.DMA((2 * times + 1,))],
        compiler_params=pltpu.CompilerParams(vmem_limit_bytes=KERNEL_VMEM),
        name="restrict",
    )(in_hbm(fine), in_hbm(null), in_hbm(operator))


def prolong(column, null_ref, out_ref, held, done):
    coarse_y = len(column) // CZ
    times, _, _, rhs, sites = held.shape
    vectors = null_ref.shape[3]
    ids = aggregate_ids((2 * vectors, sites), coarse_y)
    masks = [(lax.rem(ids, CZ) == z).astype(jnp.float32).astype(jnp.bfloat16) for z in range(CZ)]
    rows = aggregate_ids((2 * rhs, sites), coarse_y) // CZ
    mixers = []
    for h in range(2):
        mixer = []
        for y in range(coarse_y):
            real = [column[y * CZ + z][:, h * vectors : (h + 1) * vectors] for z in range(CZ)]
            imag = [column[y * CZ + z][:, (2 + h) * vectors : (3 + h) * vectors] for z in range(CZ)]
            mixer.append(jnp.concatenate([part for z in range(CZ) for part in (real[z], -imag[z])], axis=1))
            mixer.append(jnp.concatenate([part for z in range(CZ) for part in (imag[z], real[z])], axis=1))
        mixers.append(jnp.concatenate(mixer, axis=0))
    copies = []
    for t in range(times):
        for c in range(12):
            null = jnp.concatenate([null_ref[t, 0, c], null_ref[t, 1, c]], axis=0)
            null = jnp.concatenate([null * mask for mask in masks], axis=0)
            every = jnp.dot(mixers[c // 6], null, preferred_element_type=jnp.float32)
            result = every[: 2 * rhs]
            for y in range(1, coarse_y):
                result = jnp.where(rows == y, every[y * 2 * rhs : (y + 1) * 2 * rhs], result)
            result = result.astype(held.dtype)
            held[t, 0, c] = result[:rhs]
            held[t, 1, c] = result[rhs:]
        copies.append(pltpu.make_async_copy(held.at[t], out_ref.at[t], done.at[t]))
        copies[-1].start()
    for copy in copies:
        copy.wait()


def time_sides(even_slice):
    parity = lax.rem(lax.axis_index("zt"), 2)
    if not even_slice:
        parity = 1 - parity
    return 1 + parity, 2 - parity


def for_sites(extent, body):
    for y in range(extent[0]):
        for z in range(extent[1]):
            if extent[2] <= 2:
                for x in range(extent[2]):
                    body((y, z, x))
            else:
                lax.fori_loop(0, extent[2], lambda x, c, y=y, z=z: (body((y, z, x)), c)[1], 0)


def nearby(site, extent):
    found = [site]
    for axis in range(3):
        for step in [1] if extent[axis] == 2 else [1, extent[axis] - 1]:
            moved = site[axis] + step
            moved = lax.rem(moved, extent[axis]) if axis == 2 else moved % extent[axis]
            found.append(site[:axis] + (moved,) + site[axis + 1 :])
    return found


def around(operator, site, extent):
    blocks = [operator[(0, 0) + site]]
    for axis in range(3):
        ahead, behind = operator[(0, 3 + 2 * axis) + site], operator[(0, 4 + 2 * axis) + site]
        if extent[axis] == 2:
            both = ahead.astype(jnp.float32) + behind.astype(jnp.float32)
            blocks.append(both.astype(jnp.bfloat16))
        else:
            blocks += [ahead, behind]
    return list(zip(blocks, nearby(site, extent)))


def products(pairs):
    return lax.dot_general(
        jnp.concatenate([field for _, field in pairs], axis=1),
        jnp.concatenate([block for block, _ in pairs], axis=1),
        LANES,
        preferred_element_type=jnp.float32,
    )


def packed(operator, site, times):
    blocks = [block for block, _ in around(operator, site, operator.shape[2:5])]
    blocks += [operator[(0, d) + site] for d in times]
    return jnp.concatenate([block.T for block in blocks], axis=0)


def packed_stencil(weights, site, here, times):
    extent = weights.shape[:3]
    fields = [here[near] for near in nearby(site, extent)] + [field[site] for field in times]
    depth = len(fields) * weights.shape[4]
    return jnp.dot(jnp.concatenate(fields, axis=1), weights[site][:depth], preferred_element_type=jnp.float32)


def stencil(operator, site, here, times):
    extent = operator.shape[2:5]
    pairs = [(block, here[near]) for block, near in around(operator, site, extent)]
    pairs += [(operator[(0, d) + site], field[site]) for d, field in times]
    return products(pairs)


def relaxed(value, rounded, target, sums):
    image = sums + DIAGONAL_SHIFT * rounded.astype(jnp.float32)
    return value + RELAX_WEIGHT * (target.astype(jnp.float32) - image)


def block_kernel(op_mine, op_pair, block):
    _, odd = time_sides(True)
    _, pair_odd = time_sides(False)
    first = lax.axis_index("zt") < 2

    @pl.when(first)
    def _():
        block[...] = op_pair[0, pair_odd]

    @pl.when(jnp.logical_not(first))
    def _():
        block[...] = op_mine[0, odd]


def gather_kernel(pieces, operator, *refs):
    parts, (rhs_mine, rhs_pair, start_mine, start_pair, message, part_mine) = refs[: 2 * pieces], refs[2 * pieces :]
    extent = operator.shape[2:5]
    position = lax.axis_index("xy")
    even, _ = time_sides(True)
    if pieces > 1:
        parts = (parts[3], parts[1], parts[2], parts[0])
    for whole, held in ((rhs_mine, parts[:pieces]), (rhs_pair, parts[pieces:])):
        for y in range(extent[0]):
            for z in range(extent[1]):
                for x in range(extent[2]):
                    if pieces == 1:
                        whole[y, z, x] = held[0][x, y * extent[1] + z]
                    else:
                        whole[y, z, lax.rem(position + x, pieces)] = held[x][y * extent[1] + z]

    def begin(site):
        start_mine[site] = (RELAX_WEIGHT * rhs_mine[site].astype(jnp.float32)).astype(jnp.bfloat16)
        message[(0,) + site] = start_mine[site]
        start_pair[site] = (RELAX_WEIGHT * rhs_pair[site].astype(jnp.float32)).astype(jnp.bfloat16)

    for_sites(extent, begin)
    here = start_mine

    def step(site):
        sums = stencil(operator, site, here, [(even, start_pair)])
        value = RELAX_WEIGHT * rhs_mine[site].astype(jnp.float32)
        part = relaxed(value, here[site], rhs_mine[site], sums)
        part_mine[site] = part
        message[(1,) + site] = part.astype(jnp.bfloat16)

    for_sites(extent, step)


def first_pair_kernel(
    op_mine, op_pair, rhs_mine, rhs_pair, here, other, sent, part_mine,
    packed_mine, packed_pair, rest, through_near, through_pair, part_pair,
):
    sides, pair_sides = time_sides(True), time_sides(False)

    def step(site):
        packed_mine[site] = packed(op_mine, site, sides)
        packed_pair[site] = packed(op_pair, site, pair_sides)
        sums = packed_stencil(packed_pair, site, here, [other])
        value = RELAX_WEIGHT * rhs_pair[site].astype(jnp.float32)
        part_pair[site] = relaxed(value, here[site], rhs_pair[site], sums).astype(jnp.bfloat16)
        outer, inner = packed_pair[site][side_rows(packed_pair, 1)], packed_mine[site][side_rows(packed_mine, 2)]
        through_pair[site] = two_steps(outer, inner).astype(jnp.bfloat16)

    extent = op_mine.shape[2:5]
    columns = op_mine.shape[6]
    mine = sent.at[1]
    for_sites(extent, step)

    def ahead(site):
        sums = packed_stencil(packed_mine, site, mine, [part_pair])
        rest[site] = relaxed(part_mine[site], mine[site], rhs_mine[site], sums)
        for index, near in enumerate(nearby(site, extent)):
            side = packed_mine[near][side_rows(packed_mine, 1)]
            block = two_steps(side, packed_mine[site][index * columns : (index + 1) * columns])
            if index == 0:
                kept = RELAX_WEIGHT * (1 - RELAX_WEIGHT * DIAGONAL_SHIFT)
                block = block - kept * side.astype(jnp.float32)
            through_near[site + (slice(index * columns, (index + 1) * columns),)] = block.astype(jnp.bfloat16)

    for_sites(extent, ahead)


def second_pair_kernel(
    op_mine, op_pair, back_near, rhs_mine, rhs_pair, here, other, sent, part_mine, rest, part_pair, returned,
):
    extent = op_mine.shape[:3]
    mine = sent.at[1]

    def first(site):
        sums = packed_stencil(op_pair, site, here, [other])
        part_pair[site] = relaxed(here[site].astype(jnp.float32), here[site], rhs_pair[site], sums).astype(jnp.bfloat16)
        value = -RELAX_WEIGHT * products([(back_near[site], other[site])])
        returned[site] = value.astype(jnp.bfloat16)

    for_sites(extent, first)

    def second(site):
        sums = packed_stencil(op_mine, site, mine, [part_pair, returned])
        rest[site] = relaxed(part_mine[site], mine[site], rhs_mine[site], sums)

    for_sites(extent, second)


def two_steps(first, second):
    return RELAX_WEIGHT * RELAX_WEIGHT * jnp.dot(first, second, preferred_element_type=jnp.float32)


def second_near_kernel(op_mine, through_near, back_near, sent, rest, near, value, one_near):
    extent = rest.shape[:3]
    field = near.at[0]

    def first(site):
        sums = products([(back_near[site], sent[(0,) + site])])
        one_near[site] = (near[(1,) + site].astype(jnp.float32) - RELAX_WEIGHT * sums).astype(jnp.bfloat16)

    for_sites(extent, first)

    def second(site):
        value[site] = rest[site] + answer(op_mine, through_near, field, one_near, site)

    for_sites(extent, second)


def answer(op_mine, through_near, field, one_near, site):
    fields = [field[other] for other in nearby(site, through_near.shape[:3])]
    sums = jnp.dot(jnp.concatenate(fields, axis=1), through_near[site], preferred_element_type=jnp.float32)
    return sums - RELAX_WEIGHT * side_product(one_near, op_mine, site, 1)


def second_far_kernel(through_pair, far, rest, field_mine, value_mine):
    def step(site):
        value = rest[site] + jnp.dot(far[site], through_pair[site], preferred_element_type=jnp.float32)
        value_mine[site] = value
        field_mine[site] = value.astype(jnp.bfloat16)

    for_sites(rest.shape[:3], step)


def side_rows(weights, last):
    depth, columns = weights.shape[3:]
    return slice(depth - last * columns, depth - (last - 1) * columns)


def side_product(field, weights, site, last):
    return jnp.dot(field[site], weights[site][side_rows(weights, last)], preferred_element_type=jnp.float32)


def third_own_kernel(op_mine, rhs_mine, field_mine, value_mine, rest):
    def step(site):
        sums = packed_stencil(op_mine, site, field_mine, [])
        rest[site] = relaxed(value_mine[site], field_mine[site], rhs_mine[site], sums)

    for_sites(op_mine.shape[:3], step)


def third_kernel(op_mine, rest, field_mine, field_pair, message, part_next):
    def step(site):
        part = rest[site] - RELAX_WEIGHT * side_product(field_pair, op_mine, site, 2)
        part_next[site] = part
        message[(0,) + site] = field_mine[site]
        message[(1,) + site] = part.astype(jnp.bfloat16)

    for_sites(op_mine.shape[:3], step)


def last_kernel(
    op_mine, through_near, through_pair, rest, near, far, null,
    fine_out, coarse_out, result, held, done,
):
    extent = rest.shape[:3]
    field, part = near.at[0], near.at[1]

    def step(site):
        value = rest[site] + answer(op_mine, through_near, field, part, site)
        value += jnp.dot(far[site], through_pair[site], preferred_element_type=jnp.float32)
        result[(0,) + site] = value.astype(jnp.bfloat16)

    for_sites(extent, step)
    times = held.shape[0]
    copy = pltpu.make_async_copy(result, coarse_out, done.at[times])
    copy.start()
    position = lax.axis_index("xy")
    column = [result[0, y, z, position] for y in range(extent[0]) for z in range(extent[1])]
    prolong(column, null, fine_out, held, done)
    copy.wait()


def last(shape, *operands):
    full, times = operands[3].shape, shape[0]
    return pl.pallas_call(
        last_kernel,
        in_specs=[pl.BlockSpec(memory_space=pltpu.VMEM)] * len(operands),
        out_specs=[pl.BlockSpec(memory_space=pl.ANY)] * 2,
        out_shape=[
            jax.ShapeDtypeStruct(shape, jnp.bfloat16),
            jax.ShapeDtypeStruct((1,) + full, jnp.bfloat16),
        ],
        scratch_shapes=[
            pltpu.VMEM((1,) + full, jnp.bfloat16),
            pltpu.VMEM(shape, jnp.bfloat16),
            pltpu.SemaphoreType.DMA((times + 1,)),
        ],
        compiler_params=pltpu.CompilerParams(vmem_limit_bytes=KERNEL_VMEM),
        name="last",
    )(*[in_vmem(operand) for operand in operands])


def packed_depth(operator):
    blocks = 3 + sum(1 if length == 2 else 2 for length in operator.shape[2:5])
    return blocks * operator.shape[6]


def in_hbm(array):
    return pltpu.with_memory_space_constraint(array, pltpu.HBM)


def in_vmem(array):
    return pltpu.with_memory_space_constraint(array, pltpu.VMEM)


def kernel_call(kernel, name, outs, scratch, *operands, flops=0):
    return pl.pallas_call(
        kernel,
        in_specs=[pl.BlockSpec(memory_space=pltpu.VMEM)] * len(operands),
        out_specs=[pl.BlockSpec(memory_space=pltpu.VMEM)] * len(outs),
        out_shape=[pltpu.VMEM(shape, dtype) for shape, dtype in outs],
        scratch_shapes=[pltpu.VMEM(shape, dtype) for shape, dtype in scratch],
        compiler_params=pltpu.CompilerParams(vmem_limit_bytes=KERNEL_VMEM),
        cost_estimate=pl.CostEstimate(flops=flops, bytes_accessed=0, transcendentals=0) if flops else None,
        name=name,
    )(*[in_vmem(operand) for operand in operands])


def exchange_plan():
    slices, columns = lax.axis_size("zt"), lax.axis_size("xy")
    other = [i ^ 1 for i in range(slices)]
    across = [(i + 1 if i % 2 else i - 1) % slices for i in range(slices)]

    def permutation(target, turn=0):
        return [
            (i * columns + j, target[i] * columns + (j + turn) % columns) for i in range(slices) for j in range(columns)
        ]

    def send(array, target, turn=0):
        return lax.ppermute(array, ("zt", "xy"), permutation(target, turn))

    far = [other[across[i]] for i in range(slices)]
    return send, list(range(slices)), other, across, far


def per_device(fine_vectors, null_vectors, coarse_operator):
    send, same, other, across, far = exchange_plan()
    columns = lax.axis_size("xy")
    extent = coarse_operator.shape[2:5]
    bf16, f32 = jnp.bfloat16, jnp.float32
    own, null_kept, operator = restrict(fine_vectors, null_vectors, coarse_operator)
    full = extent + own.shape[1:]
    if columns == 2:
        corner, pair, beside = send(own, other, 1), send(own, other), send(own, same, 1)
        parts = [corner, beside, pair, own]
    else:
        every = lax.all_gather(own, "xy")
        parts = [every, send(every, other)]
    op_pair = send(coarse_operator, other)
    (block,) = kernel_call(block_kernel, "block", [(operator.shape[2:], bf16)], [], operator, op_pair)
    back_near = send(block, [across[1], across[0]] + across[2:])
    rhs_mine, rhs_pair, start_mine, start_pair, sent, part_mine = kernel_call(
        functools.partial(gather_kernel, len(parts) // 2),
        "gather",
        [(full, bf16)] * 4 + [((2,) + full, bf16), (full, f32)],
        [],
        operator,
        *parts,
        flops=GATHER_FLOPS,
    )
    near_message, far_field = send(sent, across), send(start_mine, far)
    packed_shape = extent + (packed_depth(operator), operator.shape[6])
    near_shape = extent + (packed_shape[3] - 2 * packed_shape[4], packed_shape[4])
    packed_mine, packed_pair, rest, through_near, through_pair = kernel_call(
        first_pair_kernel,
        "pair_one",
        [(packed_shape, bf16), (packed_shape, bf16), (full, f32), (near_shape, bf16), (operator.shape[2:], bf16)],
        [(full, bf16)],
        operator, op_pair, rhs_mine, rhs_pair, start_pair, start_mine, sent, part_mine,
    )
    (rest,) = kernel_call(
        second_near_kernel, "second_near", [(full, f32)], [(full, bf16)],
        packed_mine, through_near, back_near, sent, rest, near_message,
    )
    field_mine, value_mine = kernel_call(
        second_far_kernel, "second_far", [(full, bf16), (full, f32)], [], through_pair, far_field, rest,
    )
    field_pair = send(field_mine, other)
    (rest,) = kernel_call(
        third_own_kernel, "third_own", [(full, f32)], [], packed_mine, rhs_mine, field_mine, value_mine,
    )
    sent, part_mine = kernel_call(
        third_kernel, "third", [((2,) + full, bf16), (full, f32)], [], packed_mine, rest, field_mine, field_pair,
    )
    near_message, far_field = send(sent, across), send(field_mine, far)
    (rest,) = kernel_call(
        second_pair_kernel, "pair_two", [(full, f32)], [(full, bf16)] * 2,
        packed_mine, packed_pair, back_near, rhs_mine, rhs_pair, field_pair, field_mine, sent, part_mine,
    )
    fine_correction, coarse_iterate = last(
        fine_vectors.shape,
        packed_mine, through_near, through_pair, rest, near_message, far_field, null_kept,
    )
    return (fine_correction, coarse_iterate)


def solution(mesh):
    return jax.shard_map(
        per_device,
        mesh=mesh,
        in_specs=(
            P("zt", None, None, None, "xy"),
            P("zt", None, None, None, "xy"),
            P("zt", None, None, None, None, None, None),
        ),
        out_specs=(P("zt", None, None, None, "xy"), P("zt", None, None, None, None, None)),
        check_vma=False,
    )
```
